32 devices in a mesh: dom: 8 (over y, x, core), grp: 4 (over z).
Axes of the slice: x: 2, y: 2, z: 4, core: 2. Of those that a mesh axis runs over, the one named last changes fastest.
Arguments:
- orbitals: float32 [512, 48, 512], P('grp', 'dom'), may hold values from -10 to 10, as said below
- potential: float32 [48, 512], P('dom'), may hold values from -2 to 2
Outputs:
- filtered: float32 [512, 48, 512], P('grp', 'dom')
- correlation: float32 [512, 512], P('grp', 'dom')
The draws below stay inside these ranges and needn't reach their ends.
Inputs may be any that keep to these rules, and one draw needn't show every extreme that they name: `orbitals`: entries of order one.
All inputs are finite; a program needn't handle non-finite values.
Results may differ from the reference program's by a relative error of at most 0.003.
Values may be sent and summed in bfloat16 or wider, within the bound.
No kernel may reach another device: no remote copies, remote signals or barrier semaphores. Data moves between devices by JAX's collectives and lax.ppermute only.
A program may use at most 64 MiB of HBM per device.

```python
import jax
import jax.numpy as jnp
from jax import lax

ORBS = 512
NX = 32
NY = 16
NPLANE = 512
NZ = 48
NCELLS = 24576


def draw_orbitals(key, part):
    keys = jax.random.split(key, 5)
    noise = jax.random.normal(keys[0], (ORBS, NZ, NPLANE), jnp.float32)
    first_amp = 0.6 * jax.random.normal(keys[1], (ORBS, 1, 1), jnp.float32)
    second_amp = 0.6 * jax.random.normal(keys[2], (ORBS, 1, 1), jnp.float32)
    first_field = jax.random.normal(keys[3], (1, NZ, NPLANE), jnp.float32)
    second_field = jax.random.normal(keys[4], (1, NZ, NPLANE), jnp.float32)
    values = noise + first_amp * first_field + second_amp * second_field
    return jnp.clip(values, -10.0, 10.0)


def block_scale(rng, shape, cuts, smallest, high):
    def one(dim, blocks):
        draws = jax.random.uniform(jax.random.fold_in(jax.random.fold_in(rng, 6), dim), (blocks,), jnp.float32, smallest / len(cuts), high / len(cuts))
        return jnp.repeat(jnp.exp(draws), shape[dim] // blocks).reshape((-1,) + (1,) * (len(shape) - dim - 1))

    factor_of = one(*cuts[0])
    for cut in cuts[1:]:
        factor_of = factor_of * one(*cut)
    return factor_of


def setup_inputs(seed: int = 0) -> dict:
    key_list = jax.random.split(jax.random.key(seed), 3)
    orbitals = draw_orbitals(jax.random.fold_in(key_list[2], 71), 0)
    potential = jnp.clip(jax.random.uniform(key_list[1], (NZ, NPLANE), jnp.float32, -2.0, 2.0) * block_scale(key_list[1], (NZ, NPLANE), ((0, 8),), -0.4, 0.0), -2.0, 2.0)
    return dict(orbitals=orbitals, potential=potential)


COEFFS = [-5369.0 / 1800.0, 12.0 / 7.0, -15.0 / 56.0, 10.0 / 189.0, -1.0 / 112.0, 2.0 / 1925.0, -1.0 / 16632.0]
CENTER = 13.0
HALF_WIDTH = 11.0


def hamiltonian(block, potential):
    laplace = 3.0 * COEFFS[0] * block
    for reach in range(1, 7):
        for axis_num in (1, 2, 3):
            laplace = laplace + COEFFS[reach] * (jnp.roll(block, reach, axis_num) + jnp.roll(block, -reach, axis_num))
    return -0.5 / 0.25 * laplace + potential[None] * block


def filter_block(block, potential):
    previous = block
    current = (hamiltonian(block, potential) - CENTER * block) / HALF_WIDTH
    for degree in range(3):
        following = 2.0 * (hamiltonian(current, potential) - CENTER * current) / HALF_WIDTH - previous
        previous = current
        current = following
    return current


def reference(orbitals, potential):
    planes = orbitals.shape[1]
    shaped = orbitals.reshape((ORBS // 16, 16, planes, NY, NX))
    field = potential.reshape((planes, NY, NX))
    filtered = lax.map(lambda block: filter_block(block, field), shaped).reshape(orbitals.shape)
    rounded = filtered.astype(jnp.bfloat16)
    flat = rounded.reshape(ORBS, -1).astype(jnp.float32)
    correlation = jnp.dot(flat, flat.T, precision=lax.Precision.HIGHEST, preferred_element_type=jnp.float32) / NCELLS
    return filtered, correlation
```

```python
import functools

import jax
import jax.numpy as jnp
import numpy as np
from jax import lax
from jax.experimental import pallas as pl
from jax.experimental.pallas import tpu as pltpu
from jax.sharding import PartitionSpec as P

NX = 32
NY = 16


COEFFS = [
    -5369.0 / 1800.0,
    12.0 / 7.0,
    -15.0 / 56.0,
    10.0 / 189.0,
    -1.0 / 112.0,
    2.0 / 1925.0,
    -1.0 / 16632.0,
]
CENTER = 13.0
HALF_WIDTH = 11.0
SCALE = -0.5 / 0.25 / HALF_WIDTH

RANGE_STEP = 25.0
RANGE_BASE = 125.0
ROWS = 8
POT_ROWS = 8
VMEM_BYTES = 48 * 1024 * 1024


def plane_stencil():
    cells = np.arange(NY * NX)
    row_of = cells // NX
    col_of = cells % NX
    row_gap = (row_of[:, None] - row_of[None, :]) % NY
    col_gap = (col_of[:, None] - col_of[None, :]) % NX
    same_row = row_of[:, None] == row_of[None, :]
    same_col = col_of[:, None] == col_of[None, :]
    stencil = np.zeros((NY * NX, NY * NX))
    for reach in range(1, 7):
        along_rows = same_col & ((row_gap == reach) | (row_gap == NY - reach))
        along_cols = same_row & ((col_gap == reach) | (col_gap == NX - reach))
        stencil += COEFFS[reach] * along_rows + COEFFS[reach] * along_cols
    return stencil


def with_sign(magnitude, value):
    return jnp.where(value < 0, -magnitude, magnitude)


def range_code(value):
    return with_sign(jnp.exp2(jnp.abs(value) * RANGE_STEP - RANGE_BASE), value).astype(jnp.bfloat16)


def range_decode(code):
    code = code.astype(jnp.float32)
    return with_sign((jnp.log2(jnp.abs(code)) + RANGE_BASE) * (1.0 / RANGE_STEP), code)


def power_code(value, squarings):
    magnitude = value
    for _ in range(squarings):
        magnitude = magnitude * magnitude
    return with_sign(magnitude, value).astype(jnp.bfloat16)


def power_decode(code, squarings):
    code = code.astype(jnp.float32)
    return with_sign(jnp.exp2(jnp.log2(jnp.abs(code)) * (0.5**squarings)), code)


def whole_call(kernel, out_shape, scratch=(), scalars=0, inputs=0, flops=0):
    return pl.pallas_call(
        kernel,
        out_shape=out_shape,
        in_specs=[pl.BlockSpec(memory_space=pltpu.SMEM)] * scalars
        + [pl.BlockSpec(memory_space=pltpu.VMEM)] * inputs,
        scratch_shapes=list(scratch),
        compiler_params=pltpu.CompilerParams(vmem_limit_bytes=VMEM_BYTES),
        cost_estimate=pl.CostEstimate(flops=flops, bytes_accessed=1 << 20, transcendentals=0),
    )


def pack_kernel(domains, place, orbitals, potential, *outs):
    planes, own, cells = orbitals.shape
    per = own // domains
    field = jnp.concatenate([potential[...], jnp.zeros((POT_ROWS - planes, cells), jnp.float32)], axis=0)
    for half in range(2):
        for gap in range(domains):
            start = pl.multiple_of((place[0] ^ gap) * per + half * ROWS, ROWS)
            rows = [orbitals[plane, pl.ds(start, ROWS)] for plane in range(planes)]
            if half == 0:
                rows.append(field)
            outs[half * domains + gap][...] = range_code(jnp.concatenate(rows, axis=0))


def filter_kernel(domains, planes, opening, place, *refs):
    coded, refs = refs[:domains], refs[domains:]
    if opening:
        (high, low), outs, refs = refs[:2], refs[2 : 2 + domains], refs[2 + domains :]
        field, *refs = refs
    else:
        (field, high, low), outs, refs = refs[:3], refs[3 : 3 + domains], refs[3 + domains :]
    first, second, halves, product = refs
    cells = coded[0].shape[1]
    total = domains * planes
    length = planes * ROWS
    for gap in range(domains):
        part = place[0] ^ gap
        value = range_decode(coded[gap][...])
        first[pl.ds(pl.multiple_of(part * length, length), length)] = value[:length]
        if opening:
            shifted = (value[length:] - CENTER) * (1.0 / HALF_WIDTH) + 3.0 * COEFFS[0] * SCALE
            field[pl.ds(pl.multiple_of(part * POT_ROWS, POT_ROWS), POT_ROWS)] = shifted

    def step(source, target, opening, closing):
        value = source[...]
        upper = value.astype(jnp.bfloat16)
        halves[0] = upper
        halves[1] = (value - upper.astype(jnp.float32)).astype(jnp.bfloat16)
        product[...] = (
            jnp.dot(halves[0], high[...], preferred_element_type=jnp.float32)
            + jnp.dot(halves[1], high[...], preferred_element_type=jnp.float32)
            + jnp.dot(halves[0], low[...], preferred_element_type=jnp.float32)
        )
        for lane in range(0, cells, 128):

            def column(plane):
                start = (plane % total) * ROWS
                return slice(start, start + ROWS), slice(lane, lane + 128)

            line = [source[column(plane)] for plane in range(total)]
            for plane in range(total):
                row = plane // planes * POT_ROWS + plane % planes
                sum_ = product[column(plane)] + field[row : row + 1, lane : lane + 128] * line[plane]
                for reach in range(1, 7):
                    sum_ += (SCALE * COEFFS[reach]) * (
                        line[(plane + reach) % total] + line[(plane - reach) % total]
                    )
                if not opening:
                    sum_ = 2.0 * sum_ - target[column(plane)]
                if closing:
                    product[column(plane)] = sum_
                else:
                    target[column(plane)] = sum_

    step(first, second, True, False)
    step(second, first, False, False)
    step(first, second, False, False)
    step(second, first, False, True)
    for gap in range(domains):
        start = pl.multiple_of((place[0] ^ gap) * length, length)
        outs[gap][...] = power_code(product[pl.ds(start, length)], 3)


def quarter_kernel(domains, groups, planes, place, spot, *refs):
    coded, outs, rounded = refs[:domains], refs[domains:-1], refs[-1]
    lanes = outs[0].shape[2]
    for gap in range(domains):
        start = pl.multiple_of((place[0] ^ gap) * ROWS, ROWS)
        value = power_decode(coded[gap][...], 3)
        for plane in range(planes):
            rounded[plane, pl.ds(start, ROWS)] = value[plane * ROWS : (plane + 1) * ROWS]
    for gap in range(groups):
        start = pl.multiple_of((spot[0] ^ gap) * lanes, lanes)
        outs[gap][...] = rounded[:, :, pl.ds(start, lanes)].astype(jnp.bfloat16)


def write_kernel(domains, planes, place, *refs):
    coded, filtered = refs[:-1], refs[-1]
    for half in range(2):
        for gap in range(domains):
            start = pl.multiple_of((place[0] ^ gap) * 2 * ROWS + half * ROWS, ROWS)
            value = power_decode(coded[half * domains + gap][...], 3)
            for plane in range(planes):
                filtered[plane, pl.ds(start, ROWS)] = value[plane * ROWS : (plane + 1) * ROWS]


def gram_kernel(domains, groups, scale, place, spot, *refs):
    quarters, outs, (rows, tile) = refs[: 2 * groups], refs[2 * groups : -2], refs[-2:]
    planes, own, lanes = quarters[0].shape
    for half in range(2):
        for gap in range(groups):
            for plane in range(planes):
                value = quarters[half * groups + gap][plane].astype(jnp.float32)
                for part in range(domains):
                    start = (spot[0] ^ gap) * (2 * own) + (2 * part + half) * ROWS
                    rows[pl.ds(pl.multiple_of(start, ROWS), ROWS), plane * lanes : (plane + 1) * lanes] = value[
                        part * ROWS : (part + 1) * ROWS
                    ]
    right = rows[...].astype(jnp.bfloat16)
    tile[...] = scale * lax.dot_general(
        right, right, (((1,), (1,)), ((), ())), preferred_element_type=jnp.float32
    )
    length = tile.shape[0] // domains
    for gap in range(domains):
        value = tile[pl.ds(pl.multiple_of((place[0] ^ gap) * length, length), length)]
        outs[gap][...] = power_code(value, 2) if gap else value


def combine_kernel(domains, groups, spot, *refs):
    parts, outs, total = refs[:domains], refs[domains:-1], refs[-1]
    sum_ = parts[0][...]
    for part in parts[1:]:
        sum_ += power_decode(part[...], 2)
    total[...] = sum_
    lanes = outs[0].shape[1]
    for gap in range(groups):
        start = pl.multiple_of((spot[0] ^ gap) * lanes, lanes)
        outs[gap][...] = total[:, pl.ds(start, lanes)]


def finish_kernel(*refs):
    sum_ = refs[0][...]
    for part in refs[1:-1]:
        sum_ += part[...]
    refs[-1][...] = sum_


def exchange(blocks, axis):
    count = len(blocks)
    return [blocks[0]] + [
        lax.ppermute(blocks[gap], axis, [(i, i ^ gap) for i in range(count)]) for gap in range(1, count)
    ]


def transposed_shards(domains, groups, orbitals, potential):
    own, planes, cells = orbitals.shape
    stencil = SCALE * plane_stencil()
    high = stencil.astype(jnp.bfloat16)
    low = jnp.asarray((stencil - high.astype(np.float64)).astype(jnp.bfloat16))
    high = jnp.asarray(high)
    place = lax.axis_index("dom").astype(jnp.int32).reshape(1)
    spot = lax.axis_index("grp").astype(jnp.int32).reshape(1)
    length = planes * ROWS
    rows = domains * length
    lanes = cells // groups
    orbs = own * groups

    def arrays(count, shape, dtype):
        return (jax.ShapeDtypeStruct(shape, dtype),) * count

    packed = whole_call(
        functools.partial(pack_kernel, domains),
        arrays(domains, (length + POT_ROWS, cells), jnp.bfloat16) + arrays(domains, (length, cells), jnp.bfloat16),
        scalars=1,
        inputs=2,
        flops=1 << 20,
    )(place, orbitals.transpose(1, 0, 2), potential)
    arrived = [exchange(packed[:domains], "dom"), exchange(packed[domains:], "dom")]
    scratch = (
        pltpu.VMEM((rows, cells), jnp.float32),
        pltpu.VMEM((rows, cells), jnp.float32),
        pltpu.VMEM((2, rows, cells), jnp.bfloat16),
        pltpu.VMEM((rows, cells), jnp.float32),
    )
    sizes = arrays(domains, (length, cells), jnp.bfloat16)
    flops = 4 * 3 * 2 * rows * cells * cells
    *opened, field = whole_call(
        functools.partial(filter_kernel, domains, planes, True),
        sizes + arrays(1, (domains * POT_ROWS, cells), jnp.float32),
        scratch,
        scalars=1,
        inputs=domains + 2,
        flops=flops,
    )(place, *arrived[0], high, low)
    opened = exchange(opened, "dom")
    closed = whole_call(
        functools.partial(filter_kernel, domains, planes, False),
        sizes,
        scratch,
        scalars=1,
        inputs=domains + 3,
        flops=flops,
    )(place, *arrived[1], field, high, low)
    closed = exchange(closed, "dom")
    quarters = []
    for coded in (opened, closed):
        quarter = whole_call(
            functools.partial(quarter_kernel, domains, groups, planes),
            arrays(groups, (planes, own // 2, lanes), jnp.bfloat16),
            (pltpu.VMEM((planes, own // 2, cells), jnp.float32),),
            scalars=2,
            inputs=domains,
            flops=1 << 24,
        )(place, spot, *coded)
        quarters += exchange(quarter, "grp")
    filtered = whole_call(
        functools.partial(write_kernel, domains, planes),
        arrays(1, (planes, own, cells), jnp.float32)[0],
        scalars=1,
        inputs=2 * domains,
        flops=1 << 24,
    )(place, *opened, *closed)
    partial = whole_call(
        functools.partial(gram_kernel, domains, groups, 1.0 / (domains * planes * cells)),
        arrays(1, (orbs // domains, orbs), jnp.float32) + arrays(domains - 1, (orbs // domains, orbs), jnp.bfloat16),
        (pltpu.VMEM((orbs, planes * lanes), jnp.float32), pltpu.VMEM((orbs, orbs), jnp.float32)),
        scalars=2,
        inputs=2 * groups,
        flops=1 << 24,
    )(place, spot, *quarters)
    partial = exchange(partial, "dom")
    combined = whole_call(
        functools.partial(combine_kernel, domains, groups),
        arrays(groups, (orbs // domains, own), jnp.float32),
        (pltpu.VMEM((orbs // domains, orbs), jnp.float32),),
        scalars=1,
        inputs=domains,
        flops=1 << 20,
    )(spot, *partial)
    combined = exchange(combined, "grp")
    columns = whole_call(
        finish_kernel, arrays(1, (orbs // domains, own), jnp.float32)[0], inputs=groups, flops=1 << 16
    )(*combined)
    return filtered.transpose(1, 0, 2), columns.T


def padded_2(cells, sides, width):
    for axis, dim in sides:
        count = lax.axis_size(axis)
        head = lax.slice_in_dim(cells, 0, width, axis=dim)
        tail = lax.slice_in_dim(cells, cells.shape[dim] - width, cells.shape[dim], axis=dim)
        cells = jnp.concatenate(
            [
                lax.ppermute(tail, axis, [(i, (i + 1) % count) for i in range(count)]),
                cells,
                lax.ppermute(head, axis, [((i + 1) % count, i) for i in range(count)]),
            ],
            axis=dim,
        )
    return cells


def hamiltonian(block, field, stencil):
    count, planes, cells = block.shape
    padded = padded_2(block, (("dom", 1),), 6)
    in_plane = jnp.dot(
        block.reshape((count * planes, cells)),
        stencil,
        precision=lax.Precision.HIGHEST,
        preferred_element_type=jnp.float32,
    ).reshape(block.shape)
    laplace = in_plane + 3.0 * COEFFS[0] * block
    for reach in range(1, 7):
        along_z = (
            padded[:, 6 + reach : 6 + reach + planes] + padded[:, 6 - reach : 6 - reach + planes]
        )
        laplace = laplace + COEFFS[reach] * along_z
    return -0.5 / 0.25 * laplace + field[None] * block


def halo_shards(orbitals, potential):
    stencil = jnp.asarray(plane_stencil().astype(np.float32))
    previous = orbitals
    current = (hamiltonian(orbitals, potential, stencil) - CENTER * orbitals) / HALF_WIDTH
    for degree in range(3):
        following = (
            2.0 * (hamiltonian(current, potential, stencil) - CENTER * current) / HALF_WIDTH
            - previous
        )
        previous = current
        current = following
    own_count = current.shape[0]
    local_cells = current.shape[1] * current.shape[2]
    total_cells = local_cells * lax.axis_size("dom")
    mine = current.astype(jnp.bfloat16).reshape(own_count, local_cells)
    tile = lax.dot_general(
        mine,
        lax.all_gather(mine, "grp", axis=0, tiled=True),
        (((1,), (1,)), ((), ())),
        preferred_element_type=jnp.float32,
    )
    summed = lax.psum_scatter(tile, "dom", scatter_dimension=1, tiled=True)
    correlation = summed / total_cells
    return (current, correlation)


def solution(mesh):
    domains, groups = mesh.shape["dom"], mesh.shape["grp"]
    in_specs = (P("grp", "dom", None), P("dom", None))
    out_specs = (P("grp", "dom", None), P("grp", "dom"))

    def shards(orbitals, potential):
        own, planes, cells = orbitals.shape
        pairs = domains & (domains - 1) == 0 and groups & (groups - 1) == 0
        fits = own == 2 * ROWS * domains and planes <= POT_ROWS and planes % 2 == 0
        if pairs and fits and cells == 128 * groups and own % 128 == 0 and own * groups % (16 * domains) == 0:
            return transposed_shards(domains, groups, orbitals, potential)
        return halo_shards(orbitals, potential)

    return jax.shard_map(shards, mesh=mesh, in_specs=in_specs, out_specs=out_specs, check_vma=False)
```

```python
import functools

import jax
import jax.numpy as jnp
import numpy as np
from jax import lax
from jax.experimental import pallas as pl
from jax.experimental.pallas import tpu as pltpu
from jax.sharding import PartitionSpec as P

NX = 32
NY = 16


COEFFS = [
    -5369.0 / 1800.0,
    12.0 / 7.0,
    -15.0 / 56.0,
    10.0 / 189.0,
    -1.0 / 112.0,
    2.0 / 1925.0,
    -1.0 / 16632.0,
]
CENTER = 13.0
HALF_WIDTH = 11.0
SCALE = -0.5 / 0.25 / HALF_WIDTH

RANGE_STEP = 25.0
RANGE_BASE = 125.0
ROWS = 8
ORBITALS = 16
POT_ROWS = 8
VMEM_BYTES = 48 * 1024 * 1024


def plane_stencil():
    cells = np.arange(NY * NX)
    row_of = cells // NX
    col_of = cells % NX
    row_gap = (row_of[:, None] - row_of[None, :]) % NY
    col_gap = (col_of[:, None] - col_of[None, :]) % NX
    same_row = row_of[:, None] == row_of[None, :]
    same_col = col_of[:, None] == col_of[None, :]
    stencil = np.zeros((NY * NX, NY * NX))
    for reach in range(1, 7):
        along_rows = same_col & ((row_gap == reach) | (row_gap == NY - reach))
        along_cols = same_row & ((col_gap == reach) | (col_gap == NX - reach))
        stencil += COEFFS[reach] * along_rows + COEFFS[reach] * along_cols
    return stencil


def with_sign(magnitude, value):
    return jnp.where(value < 0, -magnitude, magnitude)


def range_code(value):
    return with_sign(jnp.exp2(jnp.abs(value) * RANGE_STEP - RANGE_BASE), value).astype(jnp.bfloat16)


def range_decode(code):
    code = code.astype(jnp.float32)
    return with_sign((jnp.log2(jnp.abs(code)) + RANGE_BASE) * (1.0 / RANGE_STEP), code)


def power_code(value, squarings):
    magnitude = value
    for _ in range(squarings):
        magnitude = magnitude * magnitude
    return with_sign(magnitude, value).astype(jnp.bfloat16)


def power_decode(code, squarings):
    code = code.astype(jnp.float32)
    return with_sign(jnp.exp2(jnp.log2(jnp.abs(code)) * (0.5**squarings)), code)


def whole_call(kernel, out_shape, in_specs, scratch=(), flops=0):
    spaces = {"s": pltpu.SMEM, "v": pltpu.VMEM, "h": pltpu.HBM}
    return pl.pallas_call(
        kernel,
        out_shape=out_shape,
        in_specs=[pl.BlockSpec(memory_space=spaces[space]) for space in in_specs],
        scratch_shapes=list(scratch),
        compiler_params=pltpu.CompilerParams(vmem_limit_bytes=VMEM_BYTES),
        cost_estimate=pl.CostEstimate(flops=flops, bytes_accessed=1 << 20, transcendentals=0),
    )


def pack_kernel(domains, place, orbitals, potential, *refs):
    outs, (held, field, sems) = refs[:domains], refs[domains:]
    planes, own, cells = held.shape
    copies = [pltpu.make_async_copy(potential, field, sems.at[planes])]
    copies += [pltpu.make_async_copy(orbitals.at[plane], held.at[plane], sems.at[plane]) for plane in range(planes)]
    for copy in copies:
        copy.start()
    copies[0].wait()
    tail = jnp.concatenate([field[...], jnp.zeros((POT_ROWS - planes, cells), jnp.float32)], axis=0)
    for plane in range(planes):
        copies[1 + plane].wait()
        for gap in range(domains):
            start = pl.multiple_of((place[0] ^ gap) * ORBITALS, ORBITALS)
            rows = held[plane, pl.ds(start, ORBITALS)]
            if plane == planes - 1:
                rows = jnp.concatenate([rows, tail], axis=0)
            outs[gap][plane * ORBITALS : plane * ORBITALS + rows.shape[0]] = range_code(rows)


def filter_kernel(domains, planes, order, place, *refs):
    coded, weights, outs = refs[:domains], refs[domains], refs[domains + 1 : 2 * domains + 1]
    field, first, second, left, product = refs[2 * domains + 1 :]
    cells = coded[0].shape[1]
    total = domains * planes
    length = planes * ORBITALS
    for ref, gap in zip(coded, order):
        part = place[0] ^ gap
        value = range_decode(ref[...])
        for plane in range(planes):
            row = pl.multiple_of((part * planes + plane) * ROWS, ROWS)
            for half in range(2):
                start = (2 * plane + half) * ROWS
                first[half, pl.ds(row, ROWS)] = value[start : start + ROWS]
        field[pl.ds(pl.multiple_of(part * POT_ROWS, POT_ROWS), POT_ROWS)] = (
            2.0 * (value[length:] - CENTER) * (1.0 / HALF_WIDTH) + 6.0 * COEFFS[0] * SCALE
        )

    def prepare(half, source):
        value = source[half]
        upper = value.astype(jnp.bfloat16)
        left[half, :, :cells] = upper
        left[half, :, cells : 2 * cells] = (value - upper.astype(jnp.float32)).astype(jnp.bfloat16)
        left[half, :, 2 * cells :] = upper

    def multiply(half, lanes):
        product[half, :, lanes] = jnp.dot(left[half], weights[:, lanes], preferred_element_type=jnp.float32)

    def add_along_z(half, lanes, source, target, opening):
        for lane in range(lanes.start, lanes.stop, 128):

            def column(plane):
                start = (plane % total) * ROWS
                return half, slice(start, start + ROWS), slice(lane, lane + 128)

            line = [source[column(plane)] for plane in range(total)]
            for plane in range(total):
                row = plane // planes * POT_ROWS + plane % planes
                sum_ = product[column(plane)] + field[row : row + 1, lane : lane + 128] * line[plane]
                for reach in range(1, 7):
                    sum_ += (2.0 * SCALE * COEFFS[reach]) * (
                        line[(plane + reach) % total] + line[(plane - reach) % total]
                    )
                target[column(plane)] = 0.5 * sum_ if opening else sum_ - target[column(plane)]

    tiles = [slice(lane, lane + 256) for lane in range(0, cells, 256)]
    prepare(0, first)
    for lanes in tiles:
        multiply(0, lanes)
    prepare(1, first)
    for degree in range(4):
        source, target = (first, second) if degree % 2 == 0 else (second, first)
        for lanes in tiles:
            multiply(1, lanes)
            add_along_z(0, lanes, source, target, degree == 0)
        if degree < 3:
            prepare(0, target)
        for lanes in tiles:
            if degree < 3:
                multiply(0, lanes)
            add_along_z(1, lanes, source, target, degree == 0)
        if degree < 3:
            prepare(1, target)
    for gap in range(domains):
        for plane in range(planes):
            row = pl.multiple_of(((place[0] ^ gap) * planes + plane) * ROWS, ROWS)
            value = jnp.concatenate([first[half, pl.ds(row, ROWS)] for half in range(2)], axis=0)
            outs[gap][plane * ORBITALS : (plane + 1) * ORBITALS] = power_code(value, 3)


def quarter_kernel(groups, planes, spot, *refs):
    coded, outs, rounded = refs[: -groups - 1], refs[-groups - 1 : -1], refs[-1]
    lanes = outs[0].shape[2]
    for index, ref in enumerate(coded):
        value = power_decode(ref[...], 3).astype(jnp.bfloat16)
        for plane in range(planes):
            rounded[plane, index * ORBITALS : (index + 1) * ORBITALS] = value[
                plane * ORBITALS : (plane + 1) * ORBITALS
            ]
    for gap in range(groups):
        start = pl.multiple_of((spot[0] ^ gap) * lanes, lanes)
        outs[gap][...] = rounded[:, :, pl.ds(start, lanes)]


def write_kernel(planes, order, place, *refs):
    coded, filtered = refs[:-1], refs[-1]
    for ref, gap in zip(coded, order):
        start = pl.multiple_of((place[0] ^ gap) * ORBITALS, ORBITALS)
        value = power_decode(ref[...], 3)
        for plane in range(planes):
            filtered[plane, pl.ds(start, ORBITALS)] = value[plane * ORBITALS : (plane + 1) * ORBITALS]


def gram_kernel(domains, along, sets, scale, place, spot, *refs):
    quarters, (kept, sent, rows, tile) = refs[:-4], refs[-4:]
    planes, _, lanes = quarters[0].shape
    own = domains * ORBITALS
    for index, gaps in enumerate(sets):
        for turn, far in enumerate(along):
            for slot, gap in enumerate(gaps):
                start = (spot[0] ^ far) * own + (place[0] ^ gap) * ORBITALS
                start = pl.multiple_of(start, ORBITALS)
                for plane in range(planes):
                    rows[pl.ds(start, ORBITALS), plane * lanes : (plane + 1) * lanes] = quarters[
                        index * len(along) + turn
                    ][plane, slot * ORBITALS : (slot + 1) * ORBITALS]
    right = rows[...]
    tile[...] = scale * lax.dot_general(
        right, right, (((1,), (1,)), ((), ())), preferred_element_type=jnp.float32
    )
    length = tile.shape[0] // domains
    for index in range(domains // 2):
        near = pl.multiple_of((place[0] ^ (2 * index)) * length, length)
        far = pl.multiple_of((place[0] ^ (2 * index + 1)) * length, length)
        kept[index * length : (index + 1) * length] = tile[pl.ds(near, length)]
        sent[index * length : (index + 1) * length] = power_code(tile[pl.ds(far, length)], 2)


def merge_kernel(kept, came, *outs):
    length = outs[0].shape[0]
    for index, out in enumerate(outs):
        rows = slice(index * length, (index + 1) * length)
        value = kept[rows] + power_decode(came[rows], 2)
        out[...] = power_code(value, 2) if index else value


def combine_kernel(groups, spot, *refs):
    parts, outs, total = refs[: -groups - 1], refs[-groups - 1 : -1], refs[-1]
    sum_ = parts[0][...]
    for part in parts[1:]:
        sum_ += power_decode(part[...], 2)
    total[...] = sum_
    lanes = outs[0].shape[1]
    for gap in range(groups):
        start = pl.multiple_of((spot[0] ^ gap) * lanes, lanes)
        outs[gap][...] = total[:, pl.ds(start, lanes)]


def finish_kernel(*refs):
    sum_ = refs[0][...]
    for part in refs[1:-1]:
        sum_ += part[...]
    refs[-1][...] = sum_


def swap(block, axis, gap):
    count = lax.axis_size(axis)
    return lax.ppermute(block, axis, [(i, i ^ gap) for i in range(count)])


def exchange(blocks, axis, order):
    came = list(blocks)
    for gap in order:
        came[gap] = swap(blocks[gap], axis, gap)
    return came


def transposed_shards(domains, groups, orbitals, potential):
    own, planes, cells = orbitals.shape
    stencil = 2.0 * SCALE * plane_stencil()
    high = stencil.astype(jnp.bfloat16)
    low = (stencil - high.astype(np.float64)).astype(jnp.bfloat16)
    weights = jnp.asarray(np.concatenate([high, high, low], axis=0))
    place = lax.axis_index("dom").astype(jnp.int32).reshape(1)
    spot = lax.axis_index("grp").astype(jnp.int32).reshape(1)
    length = planes * ORBITALS
    half_rows = domains * planes * ROWS
    lanes = cells // groups
    orbs = own * groups
    columns = orbs // domains
    hops = lambda gap: bin(gap >> 1).count("1")
    order = sorted(range(1, domains), key=lambda gap: (-hops(gap), gap))
    along = sorted(range(1, groups), key=lambda gap: (-(gap >> 1), gap))

    def arrays(count, shape, dtype):
        return (jax.ShapeDtypeStruct(shape, dtype),) * count

    packed = whole_call(
        functools.partial(pack_kernel, domains),
        arrays(domains, (length + POT_ROWS, cells), jnp.bfloat16),
        "shh",
        (
            pltpu.VMEM((planes, own, cells), jnp.float32),
            pltpu.VMEM((planes, cells), jnp.float32),
            pltpu.SemaphoreType.DMA((planes + 1,)),
        ),
        flops=1 << 20,
    )(place, orbitals.transpose(1, 0, 2), potential)
    arrived = exchange(packed, "dom", order)
    order = [0] + order
    coded = whole_call(
        functools.partial(filter_kernel, domains, planes, order),
        arrays(domains, (length, cells), jnp.bfloat16),
        "s" + "v" * domains + "v",
        (
            pltpu.VMEM((domains * POT_ROWS, cells), jnp.float32),
            pltpu.VMEM((2, half_rows, cells), jnp.float32),
            pltpu.VMEM((2, half_rows, cells), jnp.float32),
            pltpu.VMEM((2, half_rows, 3 * cells), jnp.bfloat16),
            pltpu.VMEM((2, half_rows, cells), jnp.float32),
        ),
        flops=4 * 3 * 4 * half_rows * cells * cells,
    )(place, *[arrived[gap] for gap in order], weights)
    late = [gap for gap in order if hops(gap) == 1]
    early = [gap for gap in order if gap not in late]
    coded = exchange(coded, "dom", early[1:] + late)
    quarters = []
    for gaps in (early, late):
        quarter = whole_call(
            functools.partial(quarter_kernel, groups, planes),
            arrays(groups, (planes, len(gaps) * ORBITALS, lanes), jnp.bfloat16),
            "s" + "v" * len(gaps),
            (pltpu.VMEM((planes, len(gaps) * ORBITALS, cells), jnp.bfloat16),),
            flops=1 << 24,
        )(spot, *[coded[gap] for gap in gaps])
        if gaps is early:
            quarter = list(quarter)
            quarter[0], coded[late[0]] = lax.optimization_barrier((quarter[0], coded[late[0]]))
        quarter = exchange(quarter, "grp", along)
        quarters += [quarter[gap] for gap in [0] + along]
    filtered = whole_call(
        functools.partial(write_kernel, planes, early + late),
        arrays(1, (planes, own, cells), jnp.float32)[0],
        "s" + "v" * domains,
        flops=1 << 24,
    )(place, *[coded[gap] for gap in early + late])
    filtered, quarters[0] = lax.optimization_barrier((filtered, quarters[0]))
    kept, sent = whole_call(
        functools.partial(gram_kernel, domains, [0] + along, (early, late), 1.0 / (domains * planes * cells)),
        arrays(1, (orbs // 2, orbs), jnp.float32) + arrays(1, (orbs // 2, orbs), jnp.bfloat16),
        "ss" + "v" * len(quarters),
        (pltpu.VMEM((orbs, planes * lanes), jnp.bfloat16), pltpu.VMEM((orbs, orbs), jnp.float32)),
        flops=1 << 28,
    )(place, spot, *quarters)
    chips = domains // 2
    merged = whole_call(
        merge_kernel,
        arrays(1, (columns, orbs), jnp.float32) + arrays(chips - 1, (columns, orbs), jnp.bfloat16),
        "vv",
        flops=1 << 20,
    )(kept, swap(sent, "dom", 1))
    parts = [merged[0]] + [swap(merged[gap // 2], "dom", gap) for gap in order if gap and gap % 2 == 0]
    combined = whole_call(
        functools.partial(combine_kernel, groups),
        arrays(groups, (columns, own), jnp.float32),
        "s" + "v" * chips,
        (pltpu.VMEM((columns, orbs), jnp.float32),),
        flops=1 << 20,
    )(spot, *parts)
    combined = exchange(combined, "grp", along)
    correlation = whole_call(
        finish_kernel, arrays(1, (columns, own), jnp.float32)[0], "v" * groups, flops=1 << 16
    )(*[combined[gap] for gap in [0] + along])
    return filtered.transpose(1, 0, 2), correlation.T


def padded_2(cells, sides, width):
    for axis, dim in sides:
        count = lax.axis_size(axis)
        head = lax.slice_in_dim(cells, 0, width, axis=dim)
        tail = lax.slice_in_dim(cells, cells.shape[dim] - width, cells.shape[dim], axis=dim)
        cells = jnp.concatenate(
            [
                lax.ppermute(tail, axis, [(i, (i + 1) % count) for i in range(count)]),
                cells,
                lax.ppermute(head, axis, [((i + 1) % count, i) for i in range(count)]),
            ],
            axis=dim,
        )
    return cells


def hamiltonian(block, field, stencil):
    count, planes, cells = block.shape
    padded = padded_2(block, (("dom", 1),), 6)
    in_plane = jnp.dot(
        block.reshape((count * planes, cells)),
        stencil,
        precision=lax.Precision.HIGHEST,
        preferred_element_type=jnp.float32,
    ).reshape(block.shape)
    laplace = in_plane + 3.0 * COEFFS[0] * block
    for reach in range(1, 7):
        along_z = (
            padded[:, 6 + reach : 6 + reach + planes] + padded[:, 6 - reach : 6 - reach + planes]
        )
        laplace = laplace + COEFFS[reach] * along_z
    return -0.5 / 0.25 * laplace + field[None] * block


def halo_shards(orbitals, potential):
    stencil = jnp.asarray(plane_stencil().astype(np.float32))
    previous = orbitals
    current = (hamiltonian(orbitals, potential, stencil) - CENTER * orbitals) / HALF_WIDTH
    for degree in range(3):
        following = (
            2.0 * (hamiltonian(current, potential, stencil) - CENTER * current) / HALF_WIDTH
            - previous
        )
        previous = current
        current = following
    own_count = current.shape[0]
    local_cells = current.shape[1] * current.shape[2]
    total_cells = local_cells * lax.axis_size("dom")
    mine = current.astype(jnp.bfloat16).reshape(own_count, local_cells)
    tile = lax.dot_general(
        mine,
        lax.all_gather(mine, "grp", axis=0, tiled=True),
        (((1,), (1,)), ((), ())),
        preferred_element_type=jnp.float32,
    )
    summed = lax.psum_scatter(tile, "dom", scatter_dimension=1, tiled=True)
    correlation = summed / total_cells
    return (current, correlation)


def solution(mesh):
    domains, groups = mesh.shape["dom"], mesh.shape["grp"]
    in_specs = (P("grp", "dom", None), P("dom", None))
    out_specs = (P("grp", "dom", None), P("grp", "dom"))

    def shards(orbitals, potential):
        own, planes, cells = orbitals.shape
        pairs = domains > 1 and domains & (domains - 1) == 0 and groups & (groups - 1) == 0
        fits = own == ORBITALS * domains and own % 128 == 0 and planes <= POT_ROWS
        if pairs and fits and cells % 256 == 0 and cells == 128 * groups and own * groups % (16 * domains) == 0:
            return transposed_shards(domains, groups, orbitals, potential)
        return halo_shards(orbitals, potential)

    return jax.shard_map(shards, mesh=mesh, in_specs=in_specs, out_specs=out_specs, check_vma=False)
```

```python
import functools

import jax
import jax.numpy as jnp
import numpy as np
from jax import lax
from jax.experimental import pallas as pl
from jax.experimental.pallas import tpu as pltpu
from jax.sharding import PartitionSpec as P

NX = 32
NY = 16


COEFFS = [
    -5369.0 / 1800.0,
    12.0 / 7.0,
    -15.0 / 56.0,
    10.0 / 189.0,
    -1.0 / 112.0,
    2.0 / 1925.0,
    -1.0 / 16632.0,
]
CENTER = 13.0
HALF_WIDTH = 11.0
SCALE = -0.5 / 0.25 / HALF_WIDTH
LIFT = 240.0 / 128.0 / abs(2.0 * SCALE * COEFFS[1])

RANGE_STEP = 25.0
RANGE_BASE = 125.0
ROWS = 8
ORBITALS = 16
POT_ROWS = 8
VMEM_BYTES = 48 * 1024 * 1024


def plane_stencil():
    cells = np.arange(NY * NX)
    row_of = cells // NX
    col_of = cells % NX
    row_gap = (row_of[:, None] - row_of[None, :]) % NY
    col_gap = (col_of[:, None] - col_of[None, :]) % NX
    same_row = row_of[:, None] == row_of[None, :]
    same_col = col_of[:, None] == col_of[None, :]
    stencil = np.zeros((NY * NX, NY * NX))
    for reach in range(1, 7):
        along_rows = same_col & ((row_gap == reach) | (row_gap == NY - reach))
        along_cols = same_row & ((col_gap == reach) | (col_gap == NX - reach))
        stencil += COEFFS[reach] * along_rows + COEFFS[reach] * along_cols
    return stencil


def with_sign(magnitude, value):
    return jnp.where(value < 0, -magnitude, magnitude)


def range_code(value):
    return with_sign(jnp.exp2(jnp.abs(value) * RANGE_STEP - RANGE_BASE), value).astype(jnp.bfloat16)


def range_decode(code):
    code = code.astype(jnp.float32)
    return with_sign((jnp.log2(jnp.abs(code)) + RANGE_BASE) * (1.0 / RANGE_STEP), code)


def power_code(value, squarings):
    magnitude = value
    for _ in range(squarings):
        magnitude = magnitude * magnitude
    return with_sign(magnitude, value).astype(jnp.bfloat16)


def power_decode(code, squarings):
    code = code.astype(jnp.float32)
    return with_sign(jnp.exp2(jnp.log2(jnp.abs(code)) * (0.5**squarings)), code)


def whole_call(kernel, out_shape, in_specs, scratch=(), flops=0, grant=VMEM_BYTES):
    spaces = {"s": pltpu.SMEM, "v": pltpu.VMEM, "h": pltpu.HBM}
    return pl.pallas_call(
        kernel,
        out_shape=out_shape,
        in_specs=[pl.BlockSpec(memory_space=spaces[space]) for space in in_specs],
        scratch_shapes=list(scratch),
        compiler_params=pltpu.CompilerParams(vmem_limit_bytes=grant),
        cost_estimate=pl.CostEstimate(flops=flops, bytes_accessed=1 << 20, transcendentals=0),
    )


def pack_kernel(domains, place, orbitals, potential, *refs):
    outs, (held, field, sems) = refs[:domains], refs[domains:]
    planes, own, cells = held.shape
    copies = [pltpu.make_async_copy(potential, field, sems.at[planes])]
    copies += [pltpu.make_async_copy(orbitals.at[plane], held.at[plane], sems.at[plane]) for plane in range(planes)]
    for copy in copies:
        copy.start()
    copies[0].wait()
    tail = jnp.concatenate([field[...], jnp.zeros((POT_ROWS - planes, cells), jnp.float32)], axis=0)
    for plane in range(planes):
        copies[1 + plane].wait()
        for gap in range(domains):
            start = pl.multiple_of((place[0] ^ gap) * ORBITALS, ORBITALS)
            rows = held[plane, pl.ds(start, ORBITALS)]
            if plane == planes - 1:
                rows = jnp.concatenate([rows, tail], axis=0)
            outs[gap][plane * ORBITALS : plane * ORBITALS + rows.shape[0]] = range_code(rows)


def filter_kernel(domains, planes, order, place, *refs):
    coded, weights, outs = refs[:domains], refs[domains], refs[domains + 1 : 2 * domains + 1]
    field, first, second, left, product = refs[2 * domains + 1 :]
    cells = coded[0].shape[1]
    total = domains * planes
    length = planes * ORBITALS
    for ref, gap in zip(coded, order):
        part = place[0] ^ gap
        value = range_decode(ref[...])
        first[pl.ds(pl.multiple_of(part * length, length), length)] = value[:length]
        field[pl.ds(pl.multiple_of(part * POT_ROWS, POT_ROWS), POT_ROWS)] = LIFT * (
            2.0 * (value[length:] - CENTER) * (1.0 / HALF_WIDTH) + 6.0 * COEFFS[0] * SCALE
        )

    def step(source, target, opening):
        value = source[...]
        upper = value.astype(jnp.bfloat16)
        left[:, :cells] = upper
        left[:, cells:] = (value - upper.astype(jnp.float32)).astype(jnp.bfloat16)
        tiles = [slice(lane, lane + 256) for lane in range(0, cells, 256)]
        for lanes in tiles:
            product[:, lanes] = jnp.dot(left[...], weights[:, lanes], preferred_element_type=jnp.float32)
        for lane in range(0, cells, 128):
            for offset in range(0, ORBITALS, ROWS):

                def column(plane):
                    start = (plane % total) * ORBITALS + offset
                    return slice(start, start + ROWS), slice(lane, lane + 128)

                line = [source[column(plane)] for plane in range(total)]
                for plane in range(total):
                    row = plane // planes * POT_ROWS + plane % planes
                    sum_ = product[column(plane)] + field[row : row + 1, lane : lane + 128] * line[plane]
                    for reach in range(1, 7):
                        sum_ += (2.0 * LIFT * SCALE * COEFFS[reach]) * (
                            line[(plane + reach) % total] + line[(plane - reach) % total]
                        )
                    if opening:
                        target[column(plane)] = (0.5 / LIFT) * sum_
                    else:
                        target[column(plane)] = (1.0 / LIFT) * sum_ - target[column(plane)]

    step(first, second, True)
    step(second, first, False)
    step(first, second, False)
    step(second, first, False)
    for gap in range(domains):
        start = pl.multiple_of((place[0] ^ gap) * length, length)
        outs[gap][...] = power_code(first[pl.ds(start, length)], 3)


def quarter_kernel(groups, planes, spot, *refs):
    coded, outs, rounded = refs[: -groups - 1], refs[-groups - 1 : -1], refs[-1]
    lanes = outs[0].shape[2]
    for index, ref in enumerate(coded):
        value = power_decode(ref[...], 3).astype(jnp.bfloat16)
        for plane in range(planes):
            rounded[plane, index * ORBITALS : (index + 1) * ORBITALS] = value[
                plane * ORBITALS : (plane + 1) * ORBITALS
            ]
    for gap in range(groups):
        start = pl.multiple_of((spot[0] ^ gap) * lanes, lanes)
        outs[gap][...] = rounded[:, :, pl.ds(start, lanes)]


def write_kernel(planes, order, place, *refs):
    coded, filtered = refs[:-1], refs[-1]
    for ref, gap in zip(coded, order):
        start = pl.multiple_of((place[0] ^ gap) * ORBITALS, ORBITALS)
        value = power_decode(ref[...], 3)
        for plane in range(planes):
            filtered[plane, pl.ds(start, ORBITALS)] = value[plane * ORBITALS : (plane + 1) * ORBITALS]


def gram_kernel(domains, along, sets, scale, place, spot, *refs):
    quarters, (kept, sent, rows, tile) = refs[:-4], refs[-4:]
    planes, _, lanes = quarters[0].shape
    own = domains * ORBITALS
    for index, gaps in enumerate(sets):
        for turn, far in enumerate(along):
            for slot, gap in enumerate(gaps):
                start = (spot[0] ^ far) * own + (place[0] ^ gap) * ORBITALS
                start = pl.multiple_of(start, ORBITALS)
                for plane in range(planes):
                    rows[pl.ds(start, ORBITALS), plane * lanes : (plane + 1) * lanes] = quarters[
                        index * len(along) + turn
                    ][plane, slot * ORBITALS : (slot + 1) * ORBITALS]
    right = rows[...]
    tile[...] = scale * lax.dot_general(
        right, right, (((1,), (1,)), ((), ())), preferred_element_type=jnp.float32
    )
    length = tile.shape[0] // domains
    for index in range(domains // 2):
        near = pl.multiple_of((place[0] ^ (2 * index)) * length, length)
        far = pl.multiple_of((place[0] ^ (2 * index + 1)) * length, length)
        kept[index * length : (index + 1) * length] = tile[pl.ds(near, length)]
        sent[index * length : (index + 1) * length] = power_code(tile[pl.ds(far, length)], 2)


def merge_kernel(kept, came, *outs):
    length = outs[0].shape[0]
    for index, out in enumerate(outs):
        rows = slice(index * length, (index + 1) * length)
        value = kept[rows] + power_decode(came[rows], 2)
        out[...] = power_code(value, 2) if index else value


def combine_kernel(groups, spot, *refs):
    parts, outs, total = refs[: -groups - 1], refs[-groups - 1 : -1], refs[-1]
    sum_ = parts[0][...]
    for part in parts[1:]:
        sum_ += power_decode(part[...], 2)
    total[...] = sum_
    lanes = outs[0].shape[1]
    for gap in range(groups):
        start = pl.multiple_of((spot[0] ^ gap) * lanes, lanes)
        value = total[:, pl.ds(start, lanes)]
        outs[gap][...] = power_code(value, 2) if gap else value


def finish_kernel(*refs):
    sum_ = refs[0][...]
    for part in refs[1:-1]:
        sum_ += power_decode(part[...], 2)
    refs[-1][...] = sum_


def swap(block, axis, gap):
    count = lax.axis_size(axis)
    return lax.ppermute(block, axis, [(i, i ^ gap) for i in range(count)])


def exchange(blocks, axis, order):
    came = list(blocks)
    for gap in order:
        came[gap] = swap(blocks[gap], axis, gap)
    return came


def transposed_shards(domains, groups, orbitals, potential):
    own, planes, cells = orbitals.shape
    stencil = (2.0 * LIFT * SCALE * plane_stencil()).astype(jnp.bfloat16)
    weights = jnp.asarray(np.concatenate([stencil, stencil], axis=0))
    place = lax.axis_index("dom").astype(jnp.int32).reshape(1)
    spot = lax.axis_index("grp").astype(jnp.int32).reshape(1)
    length = planes * ORBITALS
    rows = domains * length
    lanes = cells // groups
    orbs = own * groups
    columns = orbs // domains
    hops = lambda gap: bin(gap >> 1).count("1")
    order = sorted(range(1, domains), key=lambda gap: (-hops(gap), gap))
    along = sorted(range(1, groups), key=lambda gap: (-(gap >> 1), gap))

    def arrays(count, shape, dtype):
        return (jax.ShapeDtypeStruct(shape, dtype),) * count

    packed = whole_call(
        functools.partial(pack_kernel, domains),
        arrays(domains, (length + POT_ROWS, cells), jnp.bfloat16),
        "shh",
        (
            pltpu.VMEM((planes, own, cells), jnp.float32),
            pltpu.VMEM((planes, cells), jnp.float32),
            pltpu.SemaphoreType.DMA((planes + 1,)),
        ),
        flops=1 << 20,
        grant=53 * 1024 * 1024,
    )(place, orbitals.transpose(1, 0, 2), potential)
    arrived = exchange(packed, "dom", order)
    order = [0] + order
    coded = whole_call(
        functools.partial(filter_kernel, domains, planes, order),
        arrays(domains, (length, cells), jnp.bfloat16),
        "s" + "v" * domains + "v",
        (
            pltpu.VMEM((domains * POT_ROWS, cells), jnp.float32),
            pltpu.VMEM((rows, cells), jnp.float32),
            pltpu.VMEM((rows, cells), jnp.float32),
            pltpu.VMEM((rows, 2 * cells), jnp.bfloat16),
            pltpu.VMEM((rows, cells), jnp.float32),
        ),
        flops=4 * 4 * rows * cells * cells,
    )(place, *[arrived[gap] for gap in order], weights)
    late = [gap for gap in order if hops(gap) == 1]
    early = [gap for gap in order if gap not in late]
    last = late[len(late) // 2 :]
    coded = exchange(coded, "dom", early[1:] + late[: len(late) // 2])
    quarters = []
    for gaps in (early, late):
        quarter = whole_call(
            functools.partial(quarter_kernel, groups, planes),
            arrays(groups, (planes, len(gaps) * ORBITALS, lanes), jnp.bfloat16),
            "s" + "v" * len(gaps),
            (pltpu.VMEM((planes, len(gaps) * ORBITALS, cells), jnp.bfloat16),),
            flops=1 << 24,
        )(spot, *[coded[gap] for gap in gaps])
        if gaps is early:
            quarter = list(quarter)
            held = lax.optimization_barrier((quarter[0], *[coded[gap] for gap in last]))
            quarter[0] = held[0]
            for gap, block in zip(last, held[1:]):
                coded[gap] = swap(block, "dom", gap)
        quarter = exchange(quarter, "grp", along)
        quarters += [quarter[gap] for gap in [0] + along]
    filtered = whole_call(
        functools.partial(write_kernel, planes, early + late),
        arrays(1, (planes, own, cells), jnp.float32)[0],
        "s" + "v" * domains,
        flops=1 << 24,
    )(place, *[coded[gap] for gap in early + late])
    filtered, quarters[0] = lax.optimization_barrier((filtered, quarters[0]))
    kept, sent = whole_call(
        functools.partial(gram_kernel, domains, [0] + along, (early, late), 1.0 / (domains * planes * cells)),
        arrays(1, (orbs // 2, orbs), jnp.float32) + arrays(1, (orbs // 2, orbs), jnp.bfloat16),
        "ss" + "v" * len(quarters),
        (pltpu.VMEM((orbs, planes * lanes), jnp.bfloat16), pltpu.VMEM((orbs, orbs), jnp.float32)),
        flops=1 << 28,
    )(place, spot, *quarters)
    chips = domains // 2
    merged = whole_call(
        merge_kernel,
        arrays(1, (columns, orbs), jnp.float32) + arrays(chips - 1, (columns, orbs), jnp.bfloat16),
        "vv",
        flops=1 << 20,
    )(kept, swap(sent, "dom", 1))
    parts = [merged[0]] + [swap(merged[gap // 2], "dom", gap) for gap in order if gap and gap % 2 == 0]
    combined = whole_call(
        functools.partial(combine_kernel, groups),
        arrays(1, (columns, own), jnp.float32) + arrays(groups - 1, (columns, own), jnp.bfloat16),
        "s" + "v" * chips,
        (pltpu.VMEM((columns, orbs), jnp.float32),),
        flops=1 << 20,
    )(spot, *parts)
    combined = exchange(combined, "grp", along)
    correlation = whole_call(
        finish_kernel, arrays(1, (columns, own), jnp.float32)[0], "v" * groups, flops=1 << 16
    )(*[combined[gap] for gap in [0] + along])
    return filtered.transpose(1, 0, 2), correlation.T


def padded_2(cells, sides, width):
    for axis, dim in sides:
        count = lax.axis_size(axis)
        head = lax.slice_in_dim(cells, 0, width, axis=dim)
        tail = lax.slice_in_dim(cells, cells.shape[dim] - width, cells.shape[dim], axis=dim)
        cells = jnp.concatenate(
            [
                lax.ppermute(tail, axis, [(i, (i + 1) % count) for i in range(count)]),
                cells,
                lax.ppermute(head, axis, [((i + 1) % count, i) for i in range(count)]),
            ],
            axis=dim,
        )
    return cells


def hamiltonian(block, field, stencil):
    count, planes, cells = block.shape
    padded = padded_2(block, (("dom", 1),), 6)
    in_plane = jnp.dot(
        block.reshape((count * planes, cells)),
        stencil,
        precision=lax.Precision.HIGHEST,
        preferred_element_type=jnp.float32,
    ).reshape(block.shape)
    laplace = in_plane + 3.0 * COEFFS[0] * block
    for reach in range(1, 7):
        along_z = (
            padded[:, 6 + reach : 6 + reach + planes] + padded[:, 6 - reach : 6 - reach + planes]
        )
        laplace = laplace + COEFFS[reach] * along_z
    return -0.5 / 0.25 * laplace + field[None] * block


def halo_shards(orbitals, potential):
    stencil = jnp.asarray(plane_stencil().astype(np.float32))
    previous = orbitals
    current = (hamiltonian(orbitals, potential, stencil) - CENTER * orbitals) / HALF_WIDTH
    for degree in range(3):
        following = (
            2.0 * (hamiltonian(current, potential, stencil) - CENTER * current) / HALF_WIDTH
            - previous
        )
        previous = current
        current = following
    own_count = current.shape[0]
    local_cells = current.shape[1] * current.shape[2]
    total_cells = local_cells * lax.axis_size("dom")
    mine = current.astype(jnp.bfloat16).reshape(own_count, local_cells)
    tile = lax.dot_general(
        mine,
        lax.all_gather(mine, "grp", axis=0, tiled=True),
        (((1,), (1,)), ((), ())),
        preferred_element_type=jnp.float32,
    )
    summed = lax.psum_scatter(tile, "dom", scatter_dimension=1, tiled=True)
    correlation = summed / total_cells
    return (current, correlation)


def solution(mesh):
    domains, groups = mesh.shape["dom"], mesh.shape["grp"]
    in_specs = (P("grp", "dom", None), P("dom", None))
    out_specs = (P("grp", "dom", None), P("grp", "dom"))

    def shards(orbitals, potential):
        own, planes, cells = orbitals.shape
        pairs = domains > 1 and domains & (domains - 1) == 0 and groups & (groups - 1) == 0
        fits = own == ORBITALS * domains and own % 128 == 0 and planes <= POT_ROWS
        if pairs and fits and cells % 256 == 0 and cells == 128 * groups and own * groups % (16 * domains) == 0:
            return transposed_shards(domains, groups, orbitals, potential)
        return halo_shards(orbitals, potential)

    return jax.shard_map(shards, mesh=mesh, in_specs=in_specs, out_specs=out_specs, check_vma=False)
```

```python
import functools

import jax
import jax.numpy as jnp
import numpy as np
from jax import lax
from jax.experimental import pallas as pl
from jax.experimental.pallas import tpu as pltpu
from jax.sharding import PartitionSpec as P

NX = 32
NY = 16


COEFFS = [
    -5369.0 / 1800.0,
    12.0 / 7.0,
    -15.0 / 56.0,
    10.0 / 189.0,
    -1.0 / 112.0,
    2.0 / 1925.0,
    -1.0 / 16632.0,
]
CENTER = 13.0
HALF_WIDTH = 11.0
SCALE = -0.5 / 0.25 / HALF_WIDTH
LIFT = 240.0 / 128.0 / abs(2.0 * SCALE * COEFFS[1])

RANGE_STEP = 25.0
RANGE_BASE = 125.0
ROWS = 8
ORBITALS = 16
POT_ROWS = 8
VMEM_BYTES = 48 * 1024 * 1024


def plane_stencil():
    cells = np.arange(NY * NX)
    row_of = cells // NX
    col_of = cells % NX
    row_gap = (row_of[:, None] - row_of[None, :]) % NY
    col_gap = (col_of[:, None] - col_of[None, :]) % NX
    same_row = row_of[:, None] == row_of[None, :]
    same_col = col_of[:, None] == col_of[None, :]
    stencil = np.zeros((NY * NX, NY * NX))
    for reach in range(1, 7):
        along_rows = same_col & ((row_gap == reach) | (row_gap == NY - reach))
        along_cols = same_row & ((col_gap == reach) | (col_gap == NX - reach))
        stencil += COEFFS[reach] * along_rows + COEFFS[reach] * along_cols
    return stencil


def with_sign(magnitude, value):
    return jnp.where(value < 0, -magnitude, magnitude)


def range_code(value):
    return with_sign(jnp.exp2(jnp.abs(value) * RANGE_STEP - RANGE_BASE), value).astype(jnp.bfloat16)


def range_decode(code):
    code = code.astype(jnp.float32)
    return with_sign((jnp.log2(jnp.abs(code)) + RANGE_BASE) * (1.0 / RANGE_STEP), code)


def power_code(value, squarings):
    magnitude = value
    for _ in range(squarings):
        magnitude = magnitude * magnitude
    return with_sign(magnitude, value).astype(jnp.bfloat16)


def power_decode(code, squarings):
    code = code.astype(jnp.float32)
    return with_sign(jnp.exp2(jnp.log2(jnp.abs(code)) * (0.5**squarings)), code)


def whole_call(kernel, out_shape, in_specs, scratch=(), flops=0, grant=VMEM_BYTES):
    spaces = {"s": pltpu.SMEM, "v": pltpu.VMEM, "h": pltpu.HBM}
    return pl.pallas_call(
        kernel,
        out_shape=out_shape,
        in_specs=[pl.BlockSpec(memory_space=spaces[space]) for space in in_specs],
        scratch_shapes=list(scratch),
        compiler_params=pltpu.CompilerParams(vmem_limit_bytes=grant),
        cost_estimate=pl.CostEstimate(flops=flops, bytes_accessed=1 << 20, transcendentals=0),
    )


def pack_kernel(domains, place, orbitals, potential, *refs):
    outs, (held, field, sems) = refs[:domains], refs[domains:]
    planes, own, cells = held.shape
    copies = [pltpu.make_async_copy(potential, field, sems.at[planes])]
    copies += [pltpu.make_async_copy(orbitals.at[plane], held.at[plane], sems.at[plane]) for plane in range(planes)]
    for copy in copies:
        copy.start()
    copies[0].wait()
    tail = jnp.concatenate([field[...], jnp.zeros((POT_ROWS - planes, cells), jnp.float32)], axis=0)
    for plane in range(planes):
        copies[1 + plane].wait()
        for gap in range(domains):
            start = pl.multiple_of((place[0] ^ gap) * ORBITALS, ORBITALS)
            rows = held[plane, pl.ds(start, ORBITALS)]
            if plane == planes - 1:
                rows = jnp.concatenate([rows, tail], axis=0)
            outs[gap][plane * ORBITALS : plane * ORBITALS + rows.shape[0]] = range_code(rows)


def filter_kernel(domains, planes, order, place, *refs):
    coded, weights, outs = refs[:domains], refs[domains], refs[domains + 1 : 2 * domains + 1]
    field, first, second, left, product = refs[2 * domains + 1 :]
    cells = coded[0].shape[1]
    total = domains * planes
    length = planes * ORBITALS
    for ref, gap in zip(coded, order):
        part = place[0] ^ gap
        value = range_decode(ref[...])
        first[pl.ds(pl.multiple_of(part * length, length), length)] = value[:length]
        field[pl.ds(pl.multiple_of(part * POT_ROWS, POT_ROWS), POT_ROWS)] = LIFT * (
            2.0 * (value[length:] - CENTER) * (1.0 / HALF_WIDTH) + 6.0 * COEFFS[0] * SCALE
        )

    def split(turn, rows, lanes, value):
        upper = value.astype(jnp.bfloat16)
        left[turn, rows, lanes] = upper
        lower = slice(cells + lanes.start, cells + lanes.stop)
        left[turn, rows, lower] = (value - upper.astype(jnp.float32)).astype(jnp.bfloat16)

    def step(degree, source, target):
        turn = degree % 2
        for lane in range(0, cells, 256):
            lanes = slice(lane, lane + 256)
            product[:, lanes] = jnp.dot(left[turn], weights[:, lanes], preferred_element_type=jnp.float32)
        for lane in range(0, cells, 128):
            lanes = slice(lane, lane + 128)

            def rows(plane):
                start = (plane % total) * ORBITALS
                return slice(start, start + ORBITALS)

            line = [source[rows(plane), lanes] for plane in range(-6, 6)]
            for plane in range(total):
                line = line[-12:] + [source[rows(plane + 6), lanes]]
                row = plane // planes * POT_ROWS + plane % planes
                sum_ = product[rows(plane), lanes] + field[row : row + 1, lanes] * line[6]
                for reach in range(1, 7):
                    sum_ += (2.0 * LIFT * SCALE * COEFFS[reach]) * (line[6 + reach] + line[6 - reach])
                if degree == 0:
                    value = (0.5 / LIFT) * sum_
                else:
                    value = (1.0 / LIFT) * sum_ - target[rows(plane), lanes]
                target[rows(plane), lanes] = value
                if degree < 3:
                    split(1 - turn, rows(plane), lanes, value)

    split(0, slice(0, total * ORBITALS), slice(0, cells), first[...])
    step(0, first, second)
    step(1, second, first)
    step(2, first, second)
    step(3, second, first)
    for gap in range(domains):
        start = pl.multiple_of((place[0] ^ gap) * length, length)
        outs[gap][...] = power_code(first[pl.ds(start, length)], 3)


def quarter_kernel(groups, planes, spot, *refs):
    coded, outs, rounded = refs[: -groups - 1], refs[-groups - 1 : -1], refs[-1]
    lanes = outs[0].shape[2]
    for index, ref in enumerate(coded):
        value = power_decode(ref[...], 3).astype(jnp.bfloat16)
        for plane in range(planes):
            rounded[plane, index * ORBITALS : (index + 1) * ORBITALS] = value[
                plane * ORBITALS : (plane + 1) * ORBITALS
            ]
    for gap in range(groups):
        start = pl.multiple_of((spot[0] ^ gap) * lanes, lanes)
        outs[gap][...] = rounded[:, :, pl.ds(start, lanes)]


def write_kernel(planes, order, place, *refs):
    coded, filtered = refs[:-1], refs[-1]
    for ref, gap in zip(coded, order):
        start = pl.multiple_of((place[0] ^ gap) * ORBITALS, ORBITALS)
        value = power_decode(ref[...], 3)
        for plane in range(planes):
            filtered[plane, pl.ds(start, ORBITALS)] = value[plane * ORBITALS : (plane + 1) * ORBITALS]


def gram_kernel(domains, along, sets, scale, place, spot, *refs):
    quarters, (kept, sent, rows, tile) = refs[:-4], refs[-4:]
    planes, _, lanes = quarters[0].shape
    own = domains * ORBITALS
    for index, gaps in enumerate(sets):
        for turn, far in enumerate(along):
            for slot, gap in enumerate(gaps):
                start = (spot[0] ^ far) * own + (place[0] ^ gap) * ORBITALS
                start = pl.multiple_of(start, ORBITALS)
                for plane in range(planes):
                    rows[pl.ds(start, ORBITALS), plane * lanes : (plane + 1) * lanes] = quarters[
                        index * len(along) + turn
                    ][plane, slot * ORBITALS : (slot + 1) * ORBITALS]
    right = rows[...]
    tile[...] = scale * lax.dot_general(
        right, right, (((1,), (1,)), ((), ())), preferred_element_type=jnp.float32
    )
    length = tile.shape[0] // domains
    for index in range(domains // 2):
        near = pl.multiple_of((place[0] ^ (2 * index)) * length, length)
        far = pl.multiple_of((place[0] ^ (2 * index + 1)) * length, length)
        kept[index * length : (index + 1) * length] = tile[pl.ds(near, length)]
        sent[index * length : (index + 1) * length] = power_code(tile[pl.ds(far, length)], 2)


def merge_kernel(kept, came, *outs):
    length = outs[0].shape[0]
    for index, out in enumerate(outs):
        rows = slice(index * length, (index + 1) * length)
        value = kept[rows] + power_decode(came[rows], 2)
        out[...] = power_code(value, 2) if index else value


def combine_kernel(groups, spot, *refs):
    parts, outs, total = refs[: -groups - 1], refs[-groups - 1 : -1], refs[-1]
    sum_ = parts[0][...]
    for part in parts[1:]:
        sum_ += power_decode(part[...], 2)
    total[...] = sum_
    lanes = outs[0].shape[1]
    for gap in range(groups):
        start = pl.multiple_of((spot[0] ^ gap) * lanes, lanes)
        value = total[:, pl.ds(start, lanes)]
        outs[gap][...] = power_code(value, 2) if gap else value


def finish_kernel(*refs):
    sum_ = refs[0][...]
    for part in refs[1:-1]:
        sum_ += power_decode(part[...], 2)
    refs[-1][...] = sum_


def swap(block, axis, gap):
    count = lax.axis_size(axis)
    return lax.ppermute(block, axis, [(i, i ^ gap) for i in range(count)])


def exchange(blocks, axis, order):
    came = list(blocks)
    for gap in order:
        came[gap] = swap(blocks[gap], axis, gap)
    return came


def transposed_shards(domains, groups, orbitals, potential):
    own, planes, cells = orbitals.shape
    stencil = (2.0 * LIFT * SCALE * plane_stencil()).astype(jnp.bfloat16)
    weights = jnp.asarray(np.concatenate([stencil, stencil], axis=0))
    place = lax.axis_index("dom").astype(jnp.int32).reshape(1)
    spot = lax.axis_index("grp").astype(jnp.int32).reshape(1)
    length = planes * ORBITALS
    rows = domains * length
    lanes = cells // groups
    orbs = own * groups
    columns = orbs // domains
    order = [2 * (chip ^ (chip >> 1)) + core for chip in range(domains // 2) for core in range(2)][1:]
    along = sorted(range(1, groups), key=lambda gap: (-(gap >> 1), gap))

    def arrays(count, shape, dtype):
        return (jax.ShapeDtypeStruct(shape, dtype),) * count

    packed = whole_call(
        functools.partial(pack_kernel, domains),
        arrays(domains, (length + POT_ROWS, cells), jnp.bfloat16),
        "shh",
        (
            pltpu.VMEM((planes, own, cells), jnp.float32),
            pltpu.VMEM((planes, cells), jnp.float32),
            pltpu.SemaphoreType.DMA((planes + 1,)),
        ),
        flops=1 << 20,
        grant=53 * 1024 * 1024,
    )(place, orbitals.transpose(1, 0, 2), potential)
    arrived = exchange(packed, "dom", order)
    order = [0] + order
    coded = whole_call(
        functools.partial(filter_kernel, domains, planes, order),
        arrays(domains, (length, cells), jnp.bfloat16),
        "s" + "v" * domains + "v",
        (
            pltpu.VMEM((domains * POT_ROWS, cells), jnp.float32),
            pltpu.VMEM((rows, cells), jnp.float32),
            pltpu.VMEM((rows, cells), jnp.float32),
            pltpu.VMEM((2, rows, 2 * cells), jnp.bfloat16),
            pltpu.VMEM((rows, cells), jnp.float32),
        ),
        flops=4 * 4 * rows * cells * cells,
    )(place, *[arrived[gap] for gap in order], weights)
    early, late = order[: domains // 2], order[domains // 2 :]
    coded = exchange(coded, "dom", early[1:] + late)
    quarters = []
    for gaps in (early, late):
        quarter = whole_call(
            functools.partial(quarter_kernel, groups, planes),
            arrays(groups, (planes, len(gaps) * ORBITALS, lanes), jnp.bfloat16),
            "s" + "v" * len(gaps),
            (pltpu.VMEM((planes, len(gaps) * ORBITALS, cells), jnp.bfloat16),),
            flops=1 << 24,
        )(spot, *[coded[gap] for gap in gaps])
        if gaps is early:
            quarter = list(quarter)
            quarter[0], coded[late[0]] = lax.optimization_barrier((quarter[0], coded[late[0]]))
        quarter = exchange(quarter, "grp", along)
        quarters += [quarter[gap] for gap in [0] + along]
    filtered = whole_call(
        functools.partial(write_kernel, planes, early + late),
        arrays(1, (planes, own, cells), jnp.float32)[0],
        "s" + "v" * domains,
        flops=1 << 24,
    )(place, *[coded[gap] for gap in early + late])
    filtered, quarters[0] = lax.optimization_barrier((filtered, quarters[0]))
    kept, sent = whole_call(
        functools.partial(gram_kernel, domains, [0] + along, (early, late), 1.0 / (domains * planes * cells)),
        arrays(1, (orbs // 2, orbs), jnp.float32) + arrays(1, (orbs // 2, orbs), jnp.bfloat16),
        "ss" + "v" * len(quarters),
        (pltpu.VMEM((orbs, planes * lanes), jnp.bfloat16), pltpu.VMEM((orbs, orbs), jnp.float32)),
        flops=1 << 28,
    )(place, spot, *quarters)
    chips = domains // 2
    merged = whole_call(
        merge_kernel,
        arrays(1, (columns, orbs), jnp.float32) + arrays(chips - 1, (columns, orbs), jnp.bfloat16),
        "vv",
        flops=1 << 20,
    )(kept, swap(sent, "dom", 1))
    parts = [merged[0]] + [swap(merged[gap // 2], "dom", gap) for gap in order if gap and gap % 2 == 0]
    combined = whole_call(
        functools.partial(combine_kernel, groups),
        arrays(1, (columns, own), jnp.float32) + arrays(groups - 1, (columns, own), jnp.bfloat16),
        "s" + "v" * chips,
        (pltpu.VMEM((columns, orbs), jnp.float32),),
        flops=1 << 20,
    )(spot, *parts)
    combined = exchange(combined, "grp", along)
    correlation = whole_call(
        finish_kernel, arrays(1, (columns, own), jnp.float32)[0], "v" * groups, flops=1 << 16
    )(*[combined[gap] for gap in [0] + along])
    return filtered.transpose(1, 0, 2), correlation.T


def padded_2(cells, sides, width):
    for axis, dim in sides:
        count = lax.axis_size(axis)
        head = lax.slice_in_dim(cells, 0, width, axis=dim)
        tail = lax.slice_in_dim(cells, cells.shape[dim] - width, cells.shape[dim], axis=dim)
        cells = jnp.concatenate(
            [
                lax.ppermute(tail, axis, [(i, (i + 1) % count) for i in range(count)]),
                cells,
                lax.ppermute(head, axis, [((i + 1) % count, i) for i in range(count)]),
            ],
            axis=dim,
        )
    return cells


def hamiltonian(block, field, stencil):
    count, planes, cells = block.shape
    padded = padded_2(block, (("dom", 1),), 6)
    in_plane = jnp.dot(
        block.reshape((count * planes, cells)),
        stencil,
        precision=lax.Precision.HIGHEST,
        preferred_element_type=jnp.float32,
    ).reshape(block.shape)
    laplace = in_plane + 3.0 * COEFFS[0] * block
    for reach in range(1, 7):
        along_z = (
            padded[:, 6 + reach : 6 + reach + planes] + padded[:, 6 - reach : 6 - reach + planes]
        )
        laplace = laplace + COEFFS[reach] * along_z
    return -0.5 / 0.25 * laplace + field[None] * block


def halo_shards(orbitals, potential):
    stencil = jnp.asarray(plane_stencil().astype(np.float32))
    previous = orbitals
    current = (hamiltonian(orbitals, potential, stencil) - CENTER * orbitals) / HALF_WIDTH
    for degree in range(3):
        following = (
            2.0 * (hamiltonian(current, potential, stencil) - CENTER * current) / HALF_WIDTH
            - previous
        )
        previous = current
        current = following
    own_count = current.shape[0]
    local_cells = current.shape[1] * current.shape[2]
    total_cells = local_cells * lax.axis_size("dom")
    mine = current.astype(jnp.bfloat16).reshape(own_count, local_cells)
    tile = lax.dot_general(
        mine,
        lax.all_gather(mine, "grp", axis=0, tiled=True),
        (((1,), (1,)), ((), ())),
        preferred_element_type=jnp.float32,
    )
    summed = lax.psum_scatter(tile, "dom", scatter_dimension=1, tiled=True)
    correlation = summed / total_cells
    return (current, correlation)


def solution(mesh):
    domains, groups = mesh.shape["dom"], mesh.shape["grp"]
    in_specs = (P("grp", "dom", None), P("dom", None))
    out_specs = (P("grp", "dom", None), P("grp", "dom"))

    def shards(orbitals, potential):
        own, planes, cells = orbitals.shape
        pairs = domains > 1 and domains & (domains - 1) == 0 and groups & (groups - 1) == 0
        fits = own == ORBITALS * domains and own % 128 == 0 and planes <= POT_ROWS
        if pairs and fits and cells % 256 == 0 and cells == 128 * groups and own * groups % (16 * domains) == 0:
            return transposed_shards(domains, groups, orbitals, potential)
        return halo_shards(orbitals, potential)

    return jax.shard_map(shards, mesh=mesh, in_specs=in_specs, out_specs=out_specs, check_vma=False)
```

```python
import functools

import jax
import jax.numpy as jnp
import numpy as np
from jax import lax
from jax.experimental import pallas as pl
from jax.experimental.pallas import tpu as pltpu
from jax.sharding import PartitionSpec as P

NX = 32
NY = 16


COEFFS = [
    -5369.0 / 1800.0,
    12.0 / 7.0,
    -15.0 / 56.0,
    10.0 / 189.0,
    -1.0 / 112.0,
    2.0 / 1925.0,
    -1.0 / 16632.0,
]
CENTER = 13.0
HALF_WIDTH = 11.0
SCALE = -0.5 / 0.25 / HALF_WIDTH
LIFT = 240.0 / 128.0 / abs(2.0 * SCALE * COEFFS[1])

RANGE_STEP = 25.0
RANGE_BASE = 125.0
ROWS = 8
ORBITALS = 16
POT_ROWS = 8
VMEM_BYTES = 48 * 1024 * 1024


def plane_stencil():
    cells = np.arange(NY * NX)
    row_of = cells // NX
    col_of = cells % NX
    row_gap = (row_of[:, None] - row_of[None, :]) % NY
    col_gap = (col_of[:, None] - col_of[None, :]) % NX
    same_row = row_of[:, None] == row_of[None, :]
    same_col = col_of[:, None] == col_of[None, :]
    stencil = np.zeros((NY * NX, NY * NX))
    for reach in range(1, 7):
        along_rows = same_col & ((row_gap == reach) | (row_gap == NY - reach))
        along_cols = same_row & ((col_gap == reach) | (col_gap == NX - reach))
        stencil += COEFFS[reach] * along_rows + COEFFS[reach] * along_cols
    return stencil


def with_sign(magnitude, value):
    return jnp.where(value < 0, -magnitude, magnitude)


def range_code(value):
    return with_sign(jnp.exp2(jnp.abs(value) * RANGE_STEP - RANGE_BASE), value).astype(jnp.bfloat16)


def range_decode(code):
    code = code.astype(jnp.float32)
    return with_sign((jnp.log2(jnp.abs(code)) + RANGE_BASE) * (1.0 / RANGE_STEP), code)


def power_code(value, squarings):
    magnitude = value
    for _ in range(squarings):
        magnitude = magnitude * magnitude
    return with_sign(magnitude, value).astype(jnp.bfloat16)


def power_decode(code, squarings):
    code = code.astype(jnp.float32)
    return with_sign(jnp.exp2(jnp.log2(jnp.abs(code)) * (0.5**squarings)), code)


def whole_call(kernel, out_shape, in_specs, scratch=(), flops=0, grant=VMEM_BYTES):
    spaces = {"s": pltpu.SMEM, "v": pltpu.VMEM, "h": pltpu.HBM}
    return pl.pallas_call(
        kernel,
        out_shape=out_shape,
        in_specs=[pl.BlockSpec(memory_space=spaces[space]) for space in in_specs],
        scratch_shapes=list(scratch),
        compiler_params=pltpu.CompilerParams(vmem_limit_bytes=grant),
        cost_estimate=pl.CostEstimate(flops=flops, bytes_accessed=1 << 20, transcendentals=0),
    )


def pack_kernel(domains, place, orbitals, potential, *refs):
    outs, (held, field, sems) = refs[:domains], refs[domains:]
    planes, own, cells = held.shape
    copies = [pltpu.make_async_copy(potential, field, sems.at[planes])]
    copies += [pltpu.make_async_copy(orbitals.at[plane], held.at[plane], sems.at[plane]) for plane in range(planes)]
    for copy in copies:
        copy.start()
    copies[0].wait()
    tail = jnp.concatenate([field[...], jnp.zeros((POT_ROWS - planes, cells), jnp.float32)], axis=0)
    for plane in range(planes):
        copies[1 + plane].wait()
        for gap in range(domains):
            start = pl.multiple_of((place[0] ^ gap) * ORBITALS, ORBITALS)
            rows = held[plane, pl.ds(start, ORBITALS)]
            if plane == planes - 1:
                rows = jnp.concatenate([rows, tail], axis=0)
            outs[gap][plane * ORBITALS : plane * ORBITALS + rows.shape[0]] = range_code(rows)


def filter_kernel(domains, planes, order, place, *refs):
    coded, weights, outs = refs[:domains], refs[domains], refs[domains + 1 : 2 * domains + 1]
    field, first, second, left, product = refs[2 * domains + 1 :]
    cells = coded[0].shape[1]
    total = domains * planes
    length = planes * ORBITALS
    for ref, gap in zip(coded, order):
        part = place[0] ^ gap
        value = range_decode(ref[...])
        first[pl.ds(pl.multiple_of(part * length, length), length)] = value[:length]
        field[pl.ds(pl.multiple_of(part * POT_ROWS, POT_ROWS), POT_ROWS)] = LIFT * (
            2.0 * (value[length:] - CENTER) * (1.0 / HALF_WIDTH) + 6.0 * COEFFS[0] * SCALE
        )

    def step(source, target, opening):
        value = source[...]
        upper = value.astype(jnp.bfloat16)
        left[:, :cells] = upper
        left[:, cells:] = (value - upper.astype(jnp.float32)).astype(jnp.bfloat16)
        tiles = [slice(lane, lane + 256) for lane in range(0, cells, 256)]
        for lanes in tiles:
            product[:, lanes] = jnp.dot(left[...], weights[:, lanes], preferred_element_type=jnp.float32)
        for lane in range(0, cells, 128):
            for offset in range(0, ORBITALS, ROWS):

                def column(plane):
                    start = (plane % total) * ORBITALS + offset
                    return slice(start, start + ROWS), slice(lane, lane + 128)

                line = [source[column(plane)] for plane in range(total)]
                for plane in range(total):
                    row = plane // planes * POT_ROWS + plane % planes
                    sum_ = product[column(plane)] + field[row : row + 1, lane : lane + 128] * line[plane]
                    for reach in range(1, 7):
                        sum_ += (2.0 * LIFT * SCALE * COEFFS[reach]) * (
                            line[(plane + reach) % total] + line[(plane - reach) % total]
                        )
                    if opening:
                        target[column(plane)] = (0.5 / LIFT) * sum_
                    else:
                        target[column(plane)] = (1.0 / LIFT) * sum_ - target[column(plane)]

    step(first, second, True)
    step(second, first, False)
    step(first, second, False)
    step(second, first, False)
    for gap in range(domains):
        start = pl.multiple_of((place[0] ^ gap) * length, length)
        outs[gap][...] = power_code(first[pl.ds(start, length)], 3)


def quarter_kernel(groups, planes, spot, *refs):
    coded, outs, rounded = refs[: -groups - 1], refs[-groups - 1 : -1], refs[-1]
    lanes = outs[0].shape[2]
    for index, ref in enumerate(coded):
        value = power_decode(ref[...], 3).astype(jnp.bfloat16)
        for plane in range(planes):
            rounded[plane, index * ORBITALS : (index + 1) * ORBITALS] = value[
                plane * ORBITALS : (plane + 1) * ORBITALS
            ]
    for gap in range(groups):
        start = pl.multiple_of((spot[0] ^ gap) * lanes, lanes)
        outs[gap][...] = rounded[:, :, pl.ds(start, lanes)]


def write_kernel(planes, order, place, *refs):
    coded, filtered = refs[:-1], refs[-1]
    for ref, gap in zip(coded, order):
        start = pl.multiple_of((place[0] ^ gap) * ORBITALS, ORBITALS)
        value = power_decode(ref[...], 3)
        for plane in range(planes):
            filtered[plane, pl.ds(start, ORBITALS)] = value[plane * ORBITALS : (plane + 1) * ORBITALS]


def gram_kernel(domains, along, sets, scale, place, spot, *refs):
    quarters, (kept, sent, rows, tile) = refs[:-4], refs[-4:]
    planes, _, lanes = quarters[0].shape
    own = domains * ORBITALS
    for index, gaps in enumerate(sets):
        for turn, far in enumerate(along):
            for slot, gap in enumerate(gaps):
                start = (spot[0] ^ far) * own + (place[0] ^ gap) * ORBITALS
                start = pl.multiple_of(start, ORBITALS)
                for plane in range(planes):
                    rows[pl.ds(start, ORBITALS), plane * lanes : (plane + 1) * lanes] = quarters[
                        index * len(along) + turn
                    ][plane, slot * ORBITALS : (slot + 1) * ORBITALS]
    right = rows[...]
    tile[...] = scale * lax.dot_general(
        right, right, (((1,), (1,)), ((), ())), preferred_element_type=jnp.float32
    )
    length = tile.shape[0] // domains
    for index in range(domains // 2):
        near = pl.multiple_of((place[0] ^ (2 * index)) * length, length)
        far = pl.multiple_of((place[0] ^ (2 * index + 1)) * length, length)
        kept[index * length : (index + 1) * length] = tile[pl.ds(near, length)]
        sent[index * length : (index + 1) * length] = power_code(tile[pl.ds(far, length)], 2)


def merge_kernel(kept, came, *outs):
    length = outs[0].shape[0]
    for index, out in enumerate(outs):
        rows = slice(index * length, (index + 1) * length)
        value = kept[rows] + power_decode(came[rows], 2)
        out[...] = power_code(value, 2) if index else value


def combine_kernel(kept_gaps, sent_gaps, spot, *refs):
    parts, (kept, sent, total) = refs[:-3], refs[-3:]
    sum_ = parts[0][...]
    for part in parts[1:]:
        sum_ += power_decode(part[...], 2)
    total[...] = sum_
    lanes = kept.shape[1] // len(kept_gaps)
    for slot, (near, far) in enumerate(zip(kept_gaps, sent_gaps)):
        columns = slice(slot * lanes, (slot + 1) * lanes)
        kept[:, columns] = total[:, pl.ds(pl.multiple_of((spot[0] ^ near) * lanes, lanes), lanes)]
        sent[:, columns] = power_code(total[:, pl.ds(pl.multiple_of((spot[0] ^ far) * lanes, lanes), lanes)], 2)


def halve_kernel(kept, came, *outs):
    width = outs[0].shape[1]
    value = kept[...] + power_decode(came[...], 2)
    outs[0][...] = value[:, :width]
    if len(outs) > 1:
        outs[1][...] = power_code(value[:, width:], 2)


def swap(block, axis, gap):
    count = lax.axis_size(axis)
    return lax.ppermute(block, axis, [(i, i ^ gap) for i in range(count)])


def exchange(blocks, axis, order):
    came = list(blocks)
    for gap in order:
        came[gap] = swap(blocks[gap], axis, gap)
    return came


def transposed_shards(domains, groups, orbitals, potential):
    own, planes, cells = orbitals.shape
    stencil = (2.0 * LIFT * SCALE * plane_stencil()).astype(jnp.bfloat16)
    weights = jnp.asarray(np.concatenate([stencil, stencil], axis=0))
    place = lax.axis_index("dom").astype(jnp.int32).reshape(1)
    spot = lax.axis_index("grp").astype(jnp.int32).reshape(1)
    length = planes * ORBITALS
    rows = domains * length
    lanes = cells // groups
    orbs = own * groups
    columns = orbs // domains
    hops = lambda gap: bin(gap >> 1).count("1")
    order = sorted(range(1, domains), key=lambda gap: (-hops(gap), gap))
    along = sorted(range(1, groups), key=lambda gap: (-(gap >> 1), gap))

    def arrays(count, shape, dtype):
        return (jax.ShapeDtypeStruct(shape, dtype),) * count

    packed = whole_call(
        functools.partial(pack_kernel, domains),
        arrays(domains, (length + POT_ROWS, cells), jnp.bfloat16),
        "shh",
        (
            pltpu.VMEM((planes, own, cells), jnp.float32),
            pltpu.VMEM((planes, cells), jnp.float32),
            pltpu.SemaphoreType.DMA((planes + 1,)),
        ),
        flops=1 << 20,
        grant=53 * 1024 * 1024,
    )(place, orbitals.transpose(1, 0, 2), potential)
    arrived = exchange(packed, "dom", order)
    order = [0] + order
    coded = whole_call(
        functools.partial(filter_kernel, domains, planes, order),
        arrays(domains, (length, cells), jnp.bfloat16),
        "s" + "v" * domains + "v",
        (
            pltpu.VMEM((domains * POT_ROWS, cells), jnp.float32),
            pltpu.VMEM((rows, cells), jnp.float32),
            pltpu.VMEM((rows, cells), jnp.float32),
            pltpu.VMEM((rows, 2 * cells), jnp.bfloat16),
            pltpu.VMEM((rows, cells), jnp.float32),
        ),
        flops=4 * 4 * rows * cells * cells,
    )(place, *[arrived[gap] for gap in order], weights)
    late = [gap for gap in order if hops(gap) == 1]
    early = [gap for gap in order if gap not in late]
    coded = exchange(coded, "dom", early[1:] + late)
    quarters = []
    for gaps in (early, late):
        quarter = whole_call(
            functools.partial(quarter_kernel, groups, planes),
            arrays(groups, (planes, len(gaps) * ORBITALS, lanes), jnp.bfloat16),
            "s" + "v" * len(gaps),
            (pltpu.VMEM((planes, len(gaps) * ORBITALS, cells), jnp.bfloat16),),
            flops=1 << 24,
        )(spot, *[coded[gap] for gap in gaps])
        if gaps is early:
            quarter = list(quarter)
            quarter[0], coded[late[0]] = lax.optimization_barrier((quarter[0], coded[late[0]]))
        quarter = exchange(quarter, "grp", along)
        quarters += [quarter[gap] for gap in [0] + along]
    filtered = whole_call(
        functools.partial(write_kernel, planes, early + late),
        arrays(1, (planes, own, cells), jnp.float32)[0],
        "s" + "v" * domains,
        flops=1 << 24,
    )(place, *[coded[gap] for gap in early + late])
    filtered, quarters[0] = lax.optimization_barrier((filtered, quarters[0]))
    kept, sent = whole_call(
        functools.partial(gram_kernel, domains, [0] + along, (early, late), 1.0 / (domains * planes * cells)),
        arrays(1, (orbs // 2, orbs), jnp.float32) + arrays(1, (orbs // 2, orbs), jnp.bfloat16),
        "ss" + "v" * len(quarters),
        (pltpu.VMEM((orbs, planes * lanes), jnp.bfloat16), pltpu.VMEM((orbs, orbs), jnp.float32)),
        flops=1 << 28,
    )(place, spot, *quarters)
    chips = domains // 2
    merged = whole_call(
        merge_kernel,
        arrays(1, (columns, orbs), jnp.float32) + arrays(chips - 1, (columns, orbs), jnp.bfloat16),
        "vv",
        flops=1 << 20,
    )(kept, swap(sent, "dom", 1))
    parts = [merged[0]] + [swap(merged[gap // 2], "dom", gap) for gap in order if gap and gap % 2 == 0]
    odd = [2 * gap + 1 for gap in range(groups // 2)]
    even = [2 * gap for gap in range(groups // 2)]
    width = own * groups // 2
    kept, sent = whole_call(
        functools.partial(combine_kernel, even, odd),
        arrays(1, (columns, width), jnp.float32) + arrays(1, (columns, width), jnp.bfloat16),
        "s" + "v" * chips,
        (pltpu.VMEM((columns, orbs), jnp.float32),),
        flops=1 << 20,
    )(spot, *parts)
    gap = 1
    while True:
        came = swap(sent, "grp", gap)
        gap *= 2
        if gap == groups:
            break
        width //= 2
        kept, sent = whole_call(
            halve_kernel,
            arrays(1, (columns, width), jnp.float32) + arrays(1, (columns, width), jnp.bfloat16),
            "vv",
            flops=1 << 18,
        )(kept, came)
    correlation = whole_call(halve_kernel, arrays(1, (columns, own), jnp.float32), "vv", flops=1 << 16)(kept, came)[0]
    return filtered.transpose(1, 0, 2), correlation.T


def padded_2(cells, sides, width):
    for axis, dim in sides:
        count = lax.axis_size(axis)
        head = lax.slice_in_dim(cells, 0, width, axis=dim)
        tail = lax.slice_in_dim(cells, cells.shape[dim] - width, cells.shape[dim], axis=dim)
        cells = jnp.concatenate(
            [
                lax.ppermute(tail, axis, [(i, (i + 1) % count) for i in range(count)]),
                cells,
                lax.ppermute(head, axis, [((i + 1) % count, i) for i in range(count)]),
            ],
            axis=dim,
        )
    return cells


def hamiltonian(block, field, stencil):
    count, planes, cells = block.shape
    padded = padded_2(block, (("dom", 1),), 6)
    in_plane = jnp.dot(
        block.reshape((count * planes, cells)),
        stencil,
        precision=lax.Precision.HIGHEST,
        preferred_element_type=jnp.float32,
    ).reshape(block.shape)
    laplace = in_plane + 3.0 * COEFFS[0] * block
    for reach in range(1, 7):
        along_z = (
            padded[:, 6 + reach : 6 + reach + planes] + padded[:, 6 - reach : 6 - reach + planes]
        )
        laplace = laplace + COEFFS[reach] * along_z
    return -0.5 / 0.25 * laplace + field[None] * block


def halo_shards(orbitals, potential):
    stencil = jnp.asarray(plane_stencil().astype(np.float32))
    previous = orbitals
    current = (hamiltonian(orbitals, potential, stencil) - CENTER * orbitals) / HALF_WIDTH
    for degree in range(3):
        following = (
            2.0 * (hamiltonian(current, potential, stencil) - CENTER * current) / HALF_WIDTH
            - previous
        )
        previous = current
        current = following
    own_count = current.shape[0]
    local_cells = current.shape[1] * current.shape[2]
    total_cells = local_cells * lax.axis_size("dom")
    mine = current.astype(jnp.bfloat16).reshape(own_count, local_cells)
    tile = lax.dot_general(
        mine,
        lax.all_gather(mine, "grp", axis=0, tiled=True),
        (((1,), (1,)), ((), ())),
        preferred_element_type=jnp.float32,
    )
    summed = lax.psum_scatter(tile, "dom", scatter_dimension=1, tiled=True)
    correlation = summed / total_cells
    return (current, correlation)


def solution(mesh):
    domains, groups = mesh.shape["dom"], mesh.shape["grp"]
    in_specs = (P("grp", "dom", None), P("dom", None))
    out_specs = (P("grp", "dom", None), P("grp", "dom"))

    def shards(orbitals, potential):
        own, planes, cells = orbitals.shape
        pairs = domains > 1 and domains & (domains - 1) == 0 and groups & (groups - 1) == 0
        fits = own == ORBITALS * domains and own % 128 == 0 and planes <= POT_ROWS
        if pairs and fits and cells % 256 == 0 and cells == 128 * groups and own * groups % (16 * domains) == 0:
            return transposed_shards(domains, groups, orbitals, potential)
        return halo_shards(orbitals, potential)

    return jax.shard_map(shards, mesh=mesh, in_specs=in_specs, out_specs=out_specs, check_vma=False)
```

```python
import functools

import jax
import jax.numpy as jnp
import numpy as np
from jax import lax
from jax.experimental import pallas as pl
from jax.experimental.pallas import tpu as pltpu
from jax.sharding import PartitionSpec as P

NX = 32
NY = 16


COEFFS = [
    -5369.0 / 1800.0,
    12.0 / 7.0,
    -15.0 / 56.0,
    10.0 / 189.0,
    -1.0 / 112.0,
    2.0 / 1925.0,
    -1.0 / 16632.0,
]
CENTER = 13.0
HALF_WIDTH = 11.0
SCALE = -0.5 / 0.25 / HALF_WIDTH
LIFT = 240.0 / 128.0 / abs(2.0 * SCALE * COEFFS[1])

RANGE_STEP = 25.0
RANGE_BASE = 125.0
ROWS = 8
ORBITALS = 16
POT_ROWS = 8
VMEM_BYTES = 48 * 1024 * 1024


def plane_stencil():
    cells = np.arange(NY * NX)
    row_of = cells // NX
    col_of = cells % NX
    row_gap = (row_of[:, None] - row_of[None, :]) % NY
    col_gap = (col_of[:, None] - col_of[None, :]) % NX
    same_row = row_of[:, None] == row_of[None, :]
    same_col = col_of[:, None] == col_of[None, :]
    stencil = np.zeros((NY * NX, NY * NX))
    for reach in range(1, 7):
        along_rows = same_col & ((row_gap == reach) | (row_gap == NY - reach))
        along_cols = same_row & ((col_gap == reach) | (col_gap == NX - reach))
        stencil += COEFFS[reach] * along_rows + COEFFS[reach] * along_cols
    return stencil


def with_sign(magnitude, value):
    return jnp.where(value < 0, -magnitude, magnitude)


def range_code(value):
    return with_sign(jnp.exp2(jnp.abs(value) * RANGE_STEP - RANGE_BASE), value).astype(jnp.bfloat16)


def range_decode(code):
    code = code.astype(jnp.float32)
    return with_sign((jnp.log2(jnp.abs(code)) + RANGE_BASE) * (1.0 / RANGE_STEP), code)


def power_code(value, squarings):
    magnitude = value
    for _ in range(squarings):
        magnitude = magnitude * magnitude
    return with_sign(magnitude, value).astype(jnp.bfloat16)


def power_decode(code, squarings):
    code = code.astype(jnp.float32)
    return with_sign(jnp.exp2(jnp.log2(jnp.abs(code)) * (0.5**squarings)), code)


def whole_call(kernel, out_shape, in_specs, scratch=(), flops=0, grant=VMEM_BYTES):
    spaces = {"s": pltpu.SMEM, "v": pltpu.VMEM, "h": pltpu.HBM}
    return pl.pallas_call(
        kernel,
        out_shape=out_shape,
        in_specs=[pl.BlockSpec(memory_space=spaces[space]) for space in in_specs],
        scratch_shapes=list(scratch),
        compiler_params=pltpu.CompilerParams(vmem_limit_bytes=grant),
        cost_estimate=pl.CostEstimate(flops=flops, bytes_accessed=1 << 20, transcendentals=0),
    )


def pack_kernel(domains, place, orbitals, potential, *refs):
    outs, (held, field, sems) = refs[:domains], refs[domains:]
    planes, own, cells = held.shape
    copies = [pltpu.make_async_copy(potential, field, sems.at[planes])]
    copies += [pltpu.make_async_copy(orbitals.at[plane], held.at[plane], sems.at[plane]) for plane in range(planes)]
    for copy in copies:
        copy.start()
    copies[0].wait()
    tail = jnp.concatenate([field[...], jnp.zeros((POT_ROWS - planes, cells), jnp.float32)], axis=0)
    for plane in range(planes):
        copies[1 + plane].wait()
        for gap in range(domains):
            start = pl.multiple_of((place[0] ^ gap) * ORBITALS, ORBITALS)
            rows = held[plane, pl.ds(start, ORBITALS)]
            if plane == planes - 1:
                rows = jnp.concatenate([rows, tail], axis=0)
            outs[gap][plane * ORBITALS : plane * ORBITALS + rows.shape[0]] = range_code(rows)


def filter_kernel(domains, planes, order, place, *refs):
    coded, weights, outs = refs[:domains], refs[domains], refs[domains + 1 : 2 * domains + 1]
    field, first, second, left, product = refs[2 * domains + 1 :]
    cells = coded[0].shape[1]
    total = domains * planes
    length = planes * ORBITALS
    for ref, gap in zip(coded, order):
        part = place[0] ^ gap
        value = range_decode(ref[...])
        first[pl.ds(pl.multiple_of(part * length, length), length)] = value[:length]
        field[pl.ds(pl.multiple_of(part * POT_ROWS, POT_ROWS), POT_ROWS)] = LIFT * (
            2.0 * (value[length:] - CENTER) * (1.0 / HALF_WIDTH) + 6.0 * COEFFS[0] * SCALE
        )

    def step(source, target, opening):
        value = source[...]
        upper = value.astype(jnp.bfloat16)
        left[:, :cells] = upper
        left[:, cells:] = (value - upper.astype(jnp.float32)).astype(jnp.bfloat16)
        tiles = [slice(lane, lane + 256) for lane in range(0, cells, 256)]
        for lanes in tiles:
            product[:, lanes] = jnp.dot(left[...], weights[:, lanes], preferred_element_type=jnp.float32)
        for lane in range(0, cells, 128):
            for offset in range(0, ORBITALS, ROWS):

                def column(plane):
                    start = (plane % total) * ORBITALS + offset
                    return slice(start, start + ROWS), slice(lane, lane + 128)

                line = [source[column(plane)] for plane in range(total)]
                for plane in range(total):
                    row = plane // planes * POT_ROWS + plane % planes
                    sum_ = product[column(plane)] + field[row : row + 1, lane : lane + 128] * line[plane]
                    for reach in range(1, 7):
                        sum_ += (2.0 * LIFT * SCALE * COEFFS[reach]) * (
                            line[(plane + reach) % total] + line[(plane - reach) % total]
                        )
                    if opening:
                        target[column(plane)] = (0.5 / LIFT) * sum_
                    else:
                        target[column(plane)] = (1.0 / LIFT) * sum_ - target[column(plane)]

    step(first, second, True)
    step(second, first, False)
    step(first, second, False)
    step(second, first, False)
    for gap in range(domains):
        start = pl.multiple_of((place[0] ^ gap) * length, length)
        outs[gap][...] = power_code(first[pl.ds(start, length)], 3)


def quarter_kernel(groups, planes, spot, *refs):
    coded, outs, rounded = refs[: -groups - 1], refs[-groups - 1 : -1], refs[-1]
    lanes = outs[0].shape[2]
    for index, ref in enumerate(coded):
        value = power_decode(ref[...], 3).astype(jnp.bfloat16)
        for plane in range(planes):
            rounded[plane, index * ORBITALS : (index + 1) * ORBITALS] = value[
                plane * ORBITALS : (plane + 1) * ORBITALS
            ]
    for gap in range(groups):
        start = pl.multiple_of((spot[0] ^ gap) * lanes, lanes)
        outs[gap][...] = rounded[:, :, pl.ds(start, lanes)]


def write_kernel(planes, order, place, *refs):
    coded, filtered = refs[:-1], refs[-1]
    for ref, gap in zip(coded, order):
        start = pl.multiple_of((place[0] ^ gap) * ORBITALS, ORBITALS)
        value = power_decode(ref[...], 3)
        for plane in range(planes):
            filtered[plane, pl.ds(start, ORBITALS)] = value[plane * ORBITALS : (plane + 1) * ORBITALS]


def gram_kernel(domains, along, sets, scale, place, spot, *refs):
    quarters, (kept, sent, rows, tile) = refs[:-4], refs[-4:]
    planes, _, lanes = quarters[0].shape
    own = domains * ORBITALS
    for index, gaps in enumerate(sets):
        for turn, far in enumerate(along):
            for slot, gap in enumerate(gaps):
                start = (spot[0] ^ far) * own + (place[0] ^ gap) * ORBITALS
                start = pl.multiple_of(start, ORBITALS)
                for plane in range(planes):
                    rows[pl.ds(start, ORBITALS), plane * lanes : (plane + 1) * lanes] = quarters[
                        index * len(along) + turn
                    ][plane, slot * ORBITALS : (slot + 1) * ORBITALS]
    right = rows[...]
    tile[...] = scale * lax.dot_general(
        right, right, (((1,), (1,)), ((), ())), preferred_element_type=jnp.float32
    )
    length = tile.shape[0] // domains
    for index in range(domains // 2):
        near = pl.multiple_of((place[0] ^ (2 * index)) * length, length)
        far = pl.multiple_of((place[0] ^ (2 * index + 1)) * length, length)
        kept[index * length : (index + 1) * length] = tile[pl.ds(near, length)]
        sent[index * length : (index + 1) * length] = power_code(tile[pl.ds(far, length)], 2)


def merge_kernel(kept, came, *outs):
    length = outs[0].shape[0]
    for index, out in enumerate(outs):
        rows = slice(index * length, (index + 1) * length)
        value = kept[rows] + power_decode(came[rows], 2)
        out[...] = power_code(value, 2) if index else value


def combine_kernel(groups, spot, *refs):
    parts, outs, total = refs[: -groups - 1], refs[-groups - 1 : -1], refs[-1]
    sum_ = parts[0][...]
    for part in parts[1:]:
        sum_ += power_decode(part[...], 2)
    total[...] = sum_
    lanes = outs[0].shape[1]
    for gap in range(groups):
        start = pl.multiple_of((spot[0] ^ gap) * lanes, lanes)
        value = total[:, pl.ds(start, lanes)]
        outs[gap][...] = power_code(value, 2) if gap else value


def finish_kernel(*refs):
    sum_ = refs[0][...]
    for part in refs[1:-1]:
        sum_ += power_decode(part[...], 2)
    refs[-1][...] = sum_


def swap(block, axis, gap):
    count = lax.axis_size(axis)
    return lax.ppermute(block, axis, [(i, i ^ gap) for i in range(count)])


def exchange(blocks, axis, order):
    came = list(blocks)
    for gap in order:
        came[gap] = swap(blocks[gap], axis, gap)
    return came


def transposed_shards(domains, groups, orbitals, potential):
    own, planes, cells = orbitals.shape
    stencil = (2.0 * LIFT * SCALE * plane_stencil()).astype(jnp.bfloat16)
    weights = jnp.asarray(np.concatenate([stencil, stencil], axis=0))
    place = lax.axis_index("dom").astype(jnp.int32).reshape(1)
    spot = lax.axis_index("grp").astype(jnp.int32).reshape(1)
    length = planes * ORBITALS
    rows = domains * length
    lanes = cells // groups
    orbs = own * groups
    columns = orbs // domains
    hops = lambda gap: bin(gap >> 1).count("1")
    order = sorted(range(1, domains), key=lambda gap: (-hops(gap), gap))
    along = sorted(range(1, groups), key=lambda gap: (-(gap >> 1), gap))

    def arrays(count, shape, dtype):
        return (jax.ShapeDtypeStruct(shape, dtype),) * count

    packed = whole_call(
        functools.partial(pack_kernel, domains),
        arrays(domains, (length + POT_ROWS, cells), jnp.bfloat16),
        "shh",
        (
            pltpu.VMEM((planes, own, cells), jnp.float32),
            pltpu.VMEM((planes, cells), jnp.float32),
            pltpu.SemaphoreType.DMA((planes + 1,)),
        ),
        flops=1 << 20,
        grant=53 * 1024 * 1024,
    )(place, orbitals.transpose(1, 0, 2), potential)
    arrived = exchange(packed, "dom", order)
    order = [0] + order
    coded = whole_call(
        functools.partial(filter_kernel, domains, planes, order),
        arrays(domains, (length, cells), jnp.bfloat16),
        "s" + "v" * domains + "v",
        (
            pltpu.VMEM((domains * POT_ROWS, cells), jnp.float32),
            pltpu.VMEM((rows, cells), jnp.float32),
            pltpu.VMEM((rows, cells), jnp.float32),
            pltpu.VMEM((rows, 2 * cells), jnp.bfloat16),
            pltpu.VMEM((rows, cells), jnp.float32),
        ),
        flops=4 * 4 * rows * cells * cells,
    )(place, *[arrived[gap] for gap in order], weights)
    late = [gap for gap in order if hops(gap) == 1]
    early = [gap for gap in order if gap not in late]
    coded = exchange(coded, "dom", early[1:] + late)
    quarters = []
    for gaps in (early, late):
        quarter = whole_call(
            functools.partial(quarter_kernel, groups, planes),
            arrays(groups, (planes, len(gaps) * ORBITALS, lanes), jnp.bfloat16),
            "s" + "v" * len(gaps),
            (pltpu.VMEM((planes, len(gaps) * ORBITALS, cells), jnp.bfloat16),),
            flops=1 << 24,
        )(spot, *[coded[gap] for gap in gaps])
        if gaps is early:
            quarter = list(quarter)
            quarter[0], coded[late[0]] = lax.optimization_barrier((quarter[0], coded[late[0]]))
        quarter = exchange(quarter, "grp", along)
        quarters += [quarter[gap] for gap in [0] + along]
    filtered = whole_call(
        functools.partial(write_kernel, planes, early + late),
        arrays(1, (planes, own, cells), jnp.float32)[0],
        "s" + "v" * domains,
        flops=1 << 24,
    )(place, *[coded[gap] for gap in early + late])
    filtered, quarters[0] = lax.optimization_barrier((filtered, quarters[0]))
    kept, sent = whole_call(
        functools.partial(gram_kernel, domains, [0] + along, (early, late), 1.0 / (domains * planes * cells)),
        arrays(1, (orbs // 2, orbs), jnp.float32) + arrays(1, (orbs // 2, orbs), jnp.bfloat16),
        "ss" + "v" * len(quarters),
        (pltpu.VMEM((orbs, planes * lanes), jnp.bfloat16), pltpu.VMEM((orbs, orbs), jnp.float32)),
        flops=1 << 28,
    )(place, spot, *quarters)
    chips = domains // 2
    merged = whole_call(
        merge_kernel,
        arrays(1, (columns, orbs), jnp.float32) + arrays(chips - 1, (columns, orbs), jnp.bfloat16),
        "vv",
        flops=1 << 20,
    )(kept, swap(sent, "dom", 1))
    parts = [merged[0]] + [swap(merged[gap // 2], "dom", gap) for gap in order if gap and gap % 2 == 0]
    combined = whole_call(
        functools.partial(combine_kernel, groups),
        arrays(1, (columns, own), jnp.float32) + arrays(groups - 1, (columns, own), jnp.bfloat16),
        "s" + "v" * chips,
        (pltpu.VMEM((columns, orbs), jnp.float32),),
        flops=1 << 20,
    )(spot, *parts)
    combined = exchange(combined, "grp", along)
    correlation = whole_call(
        finish_kernel, arrays(1, (columns, own), jnp.float32)[0], "v" * groups, flops=1 << 16
    )(*[combined[gap] for gap in [0] + along])
    return filtered.transpose(1, 0, 2), correlation.T


def padded_2(cells, sides, width):
    for axis, dim in sides:
        count = lax.axis_size(axis)
        head = lax.slice_in_dim(cells, 0, width, axis=dim)
        tail = lax.slice_in_dim(cells, cells.shape[dim] - width, cells.shape[dim], axis=dim)
        cells = jnp.concatenate(
            [
                lax.ppermute(tail, axis, [(i, (i + 1) % count) for i in range(count)]),
                cells,
                lax.ppermute(head, axis, [((i + 1) % count, i) for i in range(count)]),
            ],
            axis=dim,
        )
    return cells


def hamiltonian(block, field, stencil):
    count, planes, cells = block.shape
    padded = padded_2(block, (("dom", 1),), 6)
    in_plane = jnp.dot(
        block.reshape((count * planes, cells)),
        stencil,
        precision=lax.Precision.HIGHEST,
        preferred_element_type=jnp.float32,
    ).reshape(block.shape)
    laplace = in_plane + 3.0 * COEFFS[0] * block
    for reach in range(1, 7):
        along_z = (
            padded[:, 6 + reach : 6 + reach + planes] + padded[:, 6 - reach : 6 - reach + planes]
        )
        laplace = laplace + COEFFS[reach] * along_z
    return -0.5 / 0.25 * laplace + field[None] * block


def halo_shards(orbitals, potential):
    stencil = jnp.asarray(plane_stencil().astype(np.float32))
    previous = orbitals
    current = (hamiltonian(orbitals, potential, stencil) - CENTER * orbitals) / HALF_WIDTH
    for degree in range(3):
        following = (
            2.0 * (hamiltonian(current, potential, stencil) - CENTER * current) / HALF_WIDTH
            - previous
        )
        previous = current
        current = following
    own_count = current.shape[0]
    local_cells = current.shape[1] * current.shape[2]
    total_cells = local_cells * lax.axis_size("dom")
    mine = current.astype(jnp.bfloat16).reshape(own_count, local_cells)
    tile = lax.dot_general(
        mine,
        lax.all_gather(mine, "grp", axis=0, tiled=True),
        (((1,), (1,)), ((), ())),
        preferred_element_type=jnp.float32,
    )
    summed = lax.psum_scatter(tile, "dom", scatter_dimension=1, tiled=True)
    correlation = summed / total_cells
    return (current, correlation)


def solution(mesh):
    domains, groups = mesh.shape["dom"], mesh.shape["grp"]
    in_specs = (P("grp", "dom", None), P("dom", None))
    out_specs = (P("grp", "dom", None), P("grp", "dom"))

    def shards(orbitals, potential):
        own, planes, cells = orbitals.shape
        pairs = domains > 1 and domains & (domains - 1) == 0 and groups & (groups - 1) == 0
        fits = own == ORBITALS * domains and own % 128 == 0 and planes <= POT_ROWS
        if pairs and fits and cells % 256 == 0 and cells == 128 * groups and own * groups % (16 * domains) == 0:
            return transposed_shards(domains, groups, orbitals, potential)
        return halo_shards(orbitals, potential)

    return jax.shard_map(shards, mesh=mesh, in_specs=in_specs, out_specs=out_specs, check_vma=False)
```
